256 devices in a mesh: rep: 8 (over z_lo, core), shard: 32 (over z_hi, x, y).
Axes of the slice: x: 4, y: 4, z: 8 (z_hi: 2, z_lo: 4; z = z_hi * 4 + z_lo), core: 2. Of those that a mesh axis runs over, the one named last changes fastest.
Arguments:
- hidden: bfloat16 [16384, 3584], P(('rep', 'shard')), may hold values from -6 to 6
- norm_gain: float32 [3584], replicated, may hold values from 0.5 to 1.5
- input_ids: int32 [16384], replicated, may hold values from 0 to 16383
- sampled_ids: int32 [16384], replicated, may hold values from 0 to 16383
- head_weight: bfloat16 [3584, 16384], P(None, 'shard'), as said below
- moment: bfloat16 [3584, 16384], P('rep', 'shard'), may hold values from -0.29882812 to 0.29882812
- curvature: bfloat16 [3584, 16384], P('rep', 'shard'), may hold values from 0.049804688 to 5
Outputs:
- moment_new: bfloat16 [3584, 16384], P('rep', 'shard')
- curvature_new: bfloat16 [3584, 16384], P('rep', 'shard')
- update_direction: bfloat16 [3584, 16384], P('rep', 'shard')
The draws below stay inside these ranges and needn't reach their ends.
Inputs may be any that keep to these rules, and one draw needn't show every extreme that they name: Entries of head_weight are finite.
All inputs are finite; a program needn't handle non-finite values.
Results may differ from the reference program's by a relative error of at most 0.039.
Values may be sent and summed in bfloat16 or wider, within the bound.
A program may use at most 192 MiB of HBM per device.

```python
import math
import jax
import jax.numpy as jnp
import numpy as np
from jax import lax

D = 3584
V = 16384
GROUP_TOK = 2048
TOKENS = 16384
N_REP = 8


def draw_head_weight(key, part):
    key = jax.random.fold_in(key, 7)
    key_entries = jax.random.fold_in(key, 0)
    key_scale = jax.random.fold_in(key, 2)
    entries = jax.random.truncated_normal(key_entries, -4.0, 4.0, (D, V), jnp.float32)
    col_scale = jnp.exp(jax.random.uniform(key_scale, (V,), jnp.float32, math.log(0.3), math.log(3.0)))
    result = col_scale * entries
    return (result * (3.0 / math.sqrt(D))).astype(jnp.bfloat16)


def with_ends(values, rng, least, top_value):
    place = [jax.random.randint(jax.random.fold_in(rng, axis), (), 0, length) for axis, length in enumerate(values.shape)]
    longest = values.shape.index(max(values.shape))
    next_to = place[:longest] + [(place[longest] + 1) % values.shape[longest]] + place[longest + 1:]
    return values.at[tuple(place)].set(least).at[tuple(next_to)].set(top_value)


def levels(rng, dims, pieces, least, high):
    factor_of, own = 1.0, jax.random.fold_in(rng, 6)
    for dim, blocks in pieces:
        steps = jnp.exp(jax.random.uniform(jax.random.fold_in(own, dim), (blocks,), jnp.float32, least / len(pieces), high / len(pieces)))
        factor_of = factor_of * jnp.repeat(steps, dims[dim] // blocks).reshape([-1 if axis == dim else 1 for axis in range(len(dims))])
    return factor_of


def cumulative_ranks(amount, slope):
    portions = [(1 << 20) // math.isqrt(grade ** slope) + 1 for grade in range(1, amount + 1)]
    scale = 1 + sum(portions) // (1 << 30)
    return np.cumsum(np.array([max(1, weight // scale) for weight in portions]))


def skewed_ids(rng, extent, count, skew):
    listing = cumulative_ranks(count, skew)
    ticket = jax.random.randint(jax.random.fold_in(rng, 1), extent, 0, int(listing[count - 1]))
    standing = jnp.searchsorted(jnp.asarray(listing, jnp.int32), ticket, side="right")
    return jax.random.permutation(jax.random.fold_in(rng, 2), count)[standing].astype(jnp.int32)


def centred(own_key, shape, spread, reach, cuts=(), kind=jnp.bfloat16):
    values = jax.random.normal(own_key, shape, jnp.float32) * spread
    if len(cuts) > 0:
        values = levels(own_key, shape, cuts, -0.22, 0.18) * values
    return jnp.clip(values, min=-reach, max=reach).astype(kind)


def setup_inputs(seed: int = 0) -> dict:
    streams_of = jax.random.split(jax.random.key(seed), 8)
    return {
        "hidden": centred(streams_of[0], (TOKENS, D), 1.0, 6.0, ((0, 256),)),
        "norm_gain": jnp.clip(1.0 + 0.1 * jax.random.normal(streams_of[1], (D,), jnp.float32), 0.5, 1.5),
        "input_ids": with_ends(skewed_ids(streams_of[2], (TOKENS,), V, 2), jax.random.fold_in(streams_of[2], 3), 0, V - 1).astype(jnp.int32),
        "sampled_ids": with_ends(skewed_ids(streams_of[3], (TOKENS,), V, 1), jax.random.fold_in(streams_of[3], 3), 0, V - 1).astype(jnp.int32),
        "head_weight": draw_head_weight(jax.random.fold_in(streams_of[7], 71), 0),
        "moment": centred(streams_of[5], (D, V), 0.05, 0.29882812, ((0, 8), (1, 32))),
        "curvature": jnp.clip(jnp.exp(math.log(5.0) - 4.609084 * jax.random.uniform(streams_of[6], (D, V), jnp.float32) ** levels(streams_of[6], (D, V), ((0, 8), (1, 32)), -0.2, 0.2)), 0.049804688, 5.0).astype(jnp.bfloat16),
    }


EPS_NORM = 1e-05
BETA_ONE = 0.96
BETA_TWO = 0.95
RHO_SCALE = 0.05

def normalize(hidden, norm_gain):
    values = hidden.astype(jnp.float32)
    row_scale = lax.rsqrt(lax.optimization_barrier(jnp.mean(values * values, axis=-1, keepdims=True)) + EPS_NORM)
    return (values * row_scale * norm_gain).astype(jnp.bfloat16)

def group_gradients(normed, token_ids, sample_ids, head_weight):
    logits = jnp.dot(normed, head_weight, preferred_element_type=jnp.float32)
    row_peak = lax.optimization_barrier(jnp.max(logits, axis=-1, keepdims=True))
    scaled_exp = jnp.exp(logits - row_peak)
    probabilities = (scaled_exp / lax.optimization_barrier(jnp.sum(scaled_exp, axis=-1, keepdims=True))).astype(jnp.bfloat16)
    shared = jnp.dot(normed.T, probabilities, preferred_element_type=jnp.float32)
    position = jnp.arange(GROUP_TOK)
    targets = jnp.where(position < GROUP_TOK - 1, jnp.roll(token_ids, -1), V).astype(jnp.int32)
    widened = normed.astype(jnp.float32)
    true_sums = jax.ops.segment_sum(widened, targets, num_segments=V + 1)[:V]
    sample_sums = jax.ops.segment_sum(widened, sample_ids, num_segments=V)
    true_part = (shared - true_sums.T).astype(jnp.bfloat16)
    sample_part = (shared - sample_sums.T).astype(jnp.bfloat16)
    return (true_part, sample_part)

def reference(hidden, norm_gain, input_ids, sampled_ids, head_weight, moment, curvature):
    normed = normalize(hidden, norm_gain).reshape(N_REP, GROUP_TOK, D)
    token_ids = input_ids.reshape(N_REP, GROUP_TOK)
    sample_ids = sampled_ids.reshape(N_REP, GROUP_TOK)

    def accumulate(running, inputs):
        true_part, sample_part = group_gradients(inputs[0], inputs[1], inputs[2], head_weight)
        return ((running[0] + true_part.astype(jnp.float32), running[1] + sample_part.astype(jnp.float32)), None)
    empty_sum = jnp.zeros((D, V), jnp.float32)
    (gradient, sample_grad), leftover = lax.scan(accumulate, (empty_sum, empty_sum), (normed, token_ids, sample_ids))
    moment_new = BETA_ONE * moment.astype(jnp.float32) + (1.0 - BETA_ONE) * gradient
    curvature_new = BETA_TWO * curvature.astype(jnp.float32) + (1.0 - BETA_TWO) * sample_grad * sample_grad
    update_direction = jnp.clip(moment_new / (RHO_SCALE * curvature_new), -1.0, 1.0)
    return (moment_new.astype(jnp.bfloat16), curvature_new.astype(jnp.bfloat16), update_direction.astype(jnp.bfloat16))
```

```python
import jax
import jax.numpy as jnp
from jax import lax
from jax.experimental import pallas as pl
from jax.experimental.pallas import tpu as pltpu
from jax.sharding import PartitionSpec as P

EPS_NORM = 1e-05
BETA_ONE = 0.96
BETA_TWO = 0.95
RHO_SCALE = 0.05

NX = NY = 4
Z_LO, Z_HI, CORES = 4, 2, 2
NZ = Z_HI * Z_LO
PLANE = NX * NY
TILES = 2 * 4
BF16, F32 = jnp.bfloat16, jnp.float32
MESH = pl.DeviceIdType.MESH


class Sizes:
    def __init__(self, rows, features, columns, state_rows):
        self.rows = rows
        self.half = rows // 2
        self.part = rows // 4
        self.features = features
        self.columns = columns
        self.tile = 4 * CORES * self.half
        self.tokens = TILES * self.tile
        self.state_rows = state_rows
        self.quarter = CORES * state_rows
        self.weight_chunks = 8


def kernel(
    sz, hidden, gain, tgt, smp, weight, moment, curvature, moment_out, curvature_out, update_out,
    normed, w_buf, w_t, expd, probs, ring, part_sum, totals, mine_out,
    st_own, st_one, st_mid, st_two, factor,
    ag_send, ag_recv, sib_send, sib_recv, w_send, w_recv, w_local, s1_send, s1_recv, s2_send, s2_recv,
    rs_send, rs_recv, fin_send, fin_recv,
):
    rep, shard = lax.axis_index("rep"), lax.axis_index("shard")
    z_lo, core = rep // CORES, rep % CORES
    z_hi, x, y = shard // PLANE, (shard // NY) % NX, shard % NY
    z = z_hi * Z_LO + z_lo
    native = core == z_hi

    def device(dx=0, dy=0, dz=0, dc=0):
        xx, yy, zz, cc = (x + dx) % NX, (y + dy) % NY, (z + dz) % NZ, (core + dc) % CORES
        return ((zz % Z_LO) * CORES + cc, (zz // Z_LO) * PLANE + xx * NY + yy)

    row_peers = [(dx, dc) for dx in range(NX) for dc in range(CORES) if (dx, dc) != (0, 0)]
    column_peers = [1, 2, 3]
    barrier = pltpu.get_barrier_semaphore()
    partners = [device(dx=dx, dc=dc) for dx, dc in row_peers]
    partners += [device(dy=dy) for dy in column_peers]
    partners += [device(dz=1), device(dz=NZ - 1)]
    for partner in partners:
        pl.semaphore_signal(barrier, inc=1, device_id=partner, device_id_type=MESH)

    def block_row(h, da, db, cc):
        a, b = (x, y) if h == 0 else (y, x)
        return ((h * 4 + (b + db) % 4) * 4 + (a + da) % 4) * (CORES * sz.half) + cc * sz.half

    w_copy = pltpu.make_async_copy(weight, w_buf, w_local)

    @pl.when(native)
    def _():
        w_copy.start()

    for h in range(2):
        values = hidden[pl.ds(h * sz.half, sz.half), :].astype(F32)
        scale = lax.rsqrt(jnp.mean(values * values, axis=-1, keepdims=True) + EPS_NORM)
        rows = pl.ds(pl.multiple_of(block_row(h, 0, 0, core), sz.half), sz.half)
        normed[rows, :] = (values * scale * gain[...]).astype(BF16)
    pl.semaphore_wait(barrier, len(partners))

    sent = []

    def start(copy):
        copy.start()
        sent.append(copy)

    def ag_copy(h, da, db, part, along, step, index):
        to_a, to_b = (step, 0) if along == 0 else (0, step)
        dx, dy = (to_a, to_b) if h == 0 else (to_b, to_a)
        first = block_row(h, da, db, core)
        if part is None:
            rows = pl.ds(pl.multiple_of(first, sz.half), sz.half)
        else:
            rows = pl.ds(pl.multiple_of(first + part * sz.part, sz.part), sz.part)
        block = normed.at[rows]
        return pltpu.make_async_remote_copy(
            src_ref=block, dst_ref=block, send_sem=ag_send.at[h, index],
            recv_sem=ag_recv.at[h, (da - to_a) % 4, (db - to_b) % 4, part or 0],
            device_id=device(dx=dx, dy=dy), device_id_type=MESH,
        )

    counts = [0, 0]

    def ag_send_block(h, da, db, part, along, step):
        start(ag_copy(h, da % 4, db % 4, part, along, step, counts[h]))
        counts[h] += 1

    def ag_wait(h, da, db):
        da, db = da % 4, db % 4
        first = block_row(h, da, db, core)
        split = da == 2 if db == 0 else db == 2
        for part in (0, 1) if split else (None,):
            if part is None:
                rows = pl.ds(pl.multiple_of(first, sz.half), sz.half)
            else:
                rows = pl.ds(pl.multiple_of(first + part * sz.part, sz.part), sz.part)
            pltpu.make_async_remote_copy(
                src_ref=normed.at[rows], dst_ref=normed.at[rows], send_sem=ag_send.at[h, 0],
                recv_sem=ag_recv.at[h, da, db, part or 0], device_id=device(dx=1), device_id_type=MESH,
            ).wait_recv()

    def sib_copy(h, da, db, cc):
        rows = pl.ds(pl.multiple_of(block_row(h, da, db, cc), sz.half), sz.half)
        return pltpu.make_async_remote_copy(
            src_ref=normed.at[rows], dst_ref=normed.at[rows], send_sem=sib_send.at[h, (da % 4) * 4 + db % 4],
            recv_sem=sib_recv.at[h, (da % 4) * 4 + db % 4], device_id=device(dc=1), device_id_type=MESH,
        )

    def to_sibling(h, da, db):
        start(sib_copy(h, da, db, core))

    chunk = sz.features // sz.weight_chunks
    up_chunks = sz.weight_chunks // 2

    def w_copy_of(way, j, source):
        rows = pl.ds((way * up_chunks + j) * chunk, chunk)
        return pltpu.make_async_remote_copy(
            src_ref=source.at[rows], dst_ref=w_buf.at[rows], send_sem=w_send.at[way, j], recv_sem=w_recv.at[way, j],
            device_id=device(dz=1 if way == 0 else NZ - 1), device_id_type=MESH,
        )

    ends = [Z_LO - 1, 0]

    def w_first():
        for way in range(2):

            @pl.when(native & (z_lo == ends[way]))
            def _():
                for j in range(up_chunks):
                    w_copy_of(way, j, weight).start()

    def w_step(j):
        @pl.when(jnp.logical_not(native))
        def _():
            for way in range(2):
                w_copy_of(way, j, w_buf).wait_recv()

                @pl.when(z_lo != ends[way])
                def _():
                    w_copy_of(way, j, w_buf).start()

    def w_finish():
        for way in range(2):

            @pl.when((native & (z_lo == ends[way])) | (jnp.logical_not(native) & (z_lo != ends[way])))
            def _():
                for j in range(up_chunks):
                    w_copy_of(way, j, w_buf).wait_send()

    def logits_tile(t):
        rows = pl.ds(pl.multiple_of(t * sz.tile, sz.tile), sz.tile)
        logits = lax.dot_general(
            w_t[...], normed[rows, :], (((1,), (1,)), ((), ())), preferred_element_type=F32
        )
        peak = jnp.max(logits, axis=0, keepdims=True)
        scaled = jnp.exp(logits - peak)
        expd[t] = scaled
        st_own[pl.ds(t, 1), :] = peak
        st_own[pl.ds(TILES + t, 1), :] = jnp.sum(scaled, axis=0, keepdims=True)

    def two_tiles(offset):
        for h in range(2):
            for da in range(4):
                sib_copy(h, da, offset, core).wait_recv()

        def body(h, carry):
            logits_tile(h * 4 + jnp.where(h == 0, y + offset, x + offset) % 4)
            return carry

        lax.fori_loop(0, 2, body, 0)

    w_first()
    for h in range(2):
        for step in (1, -1):
            ag_send_block(h, 0, 0, None, 0, step)
    for h in range(2):
        for step in (1, -1):
            ag_send_block(h, 0, 0, None, 1, step)
        to_sibling(h, 0, 0)

    def forward_a(h):
        for da in (-1, 1):
            ag_wait(h, da, 0)
            ag_send_block(h, da, 0, 0 if da == -1 else 1, 0, -da)
        for da in (-1, 1):
            for step in (1, -1):
                ag_send_block(h, da, 0, None, 1, step)
            to_sibling(h, da, 0)

    def across_a(h):
        ag_wait(h, 2, 0)
        for step in (1, -1):
            ag_send_block(h, 2, 0, None, 1, step)
        to_sibling(h, 2, 0)

    def forward_b(h, da):
        for db in (-1, 1):
            ag_wait(h, da, db)
            ag_send_block(h, da, db, 0 if db == -1 else 1, 1, -db)
            to_sibling(h, da, db)

    def across_b(h, da):
        ag_wait(h, da, 2)
        to_sibling(h, da, 2)

    for h in range(2):
        forward_a(h)
    w_step(0)
    for h in range(2):
        forward_b(h, 0)
    for h in range(2):
        across_a(h)
    w_step(1)
    for h in range(2):
        forward_b(h, -1)
    w_step(2)
    for h in range(2):
        forward_b(h, 1)
    w_step(3)
    for h in range(2):
        across_b(h, 0)

    @pl.when(native)
    def _():
        w_copy.wait()

    slab = sz.columns

    def turn(j, carry):
        first = pl.multiple_of(j * slab, slab)
        w_t[:, pl.ds(first, slab)] = w_buf[pl.ds(first, slab), :].T
        return carry

    lax.fori_loop(0, sz.features // slab, turn, 0)
    two_tiles(0)
    for h in range(2):
        forward_b(h, 2)
    two_tiles(1)
    two_tiles(-1)
    for h in range(2):
        across_b(h, -1)
        across_b(h, 1)
    for h in range(2):
        across_b(h, 2)
    two_tiles(2)

    def join(pairs):
        peak = pairs[0][0]
        for other, _ in pairs[1:]:
            peak = jnp.maximum(peak, other)
        total = 0.0
        for other, part in pairs:
            total = total + part * jnp.exp(other - peak)
        return peak, total

    def pair(ref):
        return ref[:TILES, :], ref[TILES:, :]

    ones = [
        pltpu.make_async_remote_copy(
            src_ref=st_own, dst_ref=st_one.at[j], send_sem=s1_send.at[j], recv_sem=s1_recv.at[j],
            device_id=device(dx=dx, dc=dc), device_id_type=MESH,
        )
        for j, (dx, dc) in enumerate(row_peers)
    ]
    for copy in ones:
        start(copy)
    for copy in ones:
        copy.wait_recv()
    peak, total = join([pair(st_own)] + [pair(st_one.at[j]) for j in range(len(row_peers))])
    st_mid[:TILES, :] = peak
    st_mid[TILES:, :] = total
    twos = [
        pltpu.make_async_remote_copy(
            src_ref=st_mid, dst_ref=st_two.at[j], send_sem=s2_send.at[j], recv_sem=s2_recv.at[j],
            device_id=device(dy=dy), device_id_type=MESH,
        )
        for j, dy in enumerate(column_peers)
    ]
    for copy in twos:
        start(copy)
    for copy in twos:
        copy.wait_recv()
    peak, total = join([pair(st_mid)] + [pair(st_two.at[j]) for j in range(len(column_peers))])
    factor[...] = jnp.exp(st_own[:TILES, :] - peak) / total

    def probs_tile(t, carry):
        scaled = expd[t] * factor[pl.ds(t, 1), :]
        column = lax.broadcasted_iota(jnp.int32, (sz.columns, sz.tile), 0)
        lanes = pl.ds(pl.multiple_of(t * sz.tile, sz.tile), sz.tile)
        for d, labels in enumerate((tgt, smp)):
            hit = column == labels[pl.ds(t, 1), :]
            probs[d, :, lanes] = jnp.where(hit, scaled - 1.0, scaled).astype(BF16)
        return carry

    lax.fori_loop(0, TILES, probs_tile, 0)

    sub = sz.columns // 2

    def rs_copy(d, slot, u):
        block = ring.at[d, slot, u]
        return pltpu.make_async_remote_copy(
            src_ref=block, dst_ref=block, send_sem=rs_send.at[d, slot, u], recv_sem=rs_recv.at[d, slot, u],
            device_id=device(dz=1 if d == 0 else NZ - 1), device_id_type=MESH,
        )

    def product(d, quarter):
        lanes = pl.ds(pl.multiple_of(quarter * sz.quarter, sz.quarter), sz.quarter)
        part_sum[d] = jnp.dot(probs[d], normed[:, lanes], preferred_element_type=F32)

    def owner(d, k):
        return (z + NZ - 1 - k) % NZ if d == 0 else (z + 1 + k) % NZ

    def hop(k, carry):
        for d in range(2):
            to = owner(d, k)

            @pl.when(to // Z_LO == core)
            def _():
                product(d, to % Z_LO)

        for d in range(2):
            to = owner(d, k)

            @pl.when(to // Z_LO == core)
            def _():
                slot = to % Z_LO
                for u in range(2):
                    rows = slice(u * sub, (u + 1) * sub)

                    @pl.when(k == 0)
                    def _():
                        ring[d, slot, u] = part_sum[d, rows, :].astype(BF16)

                    @pl.when(k > 0)
                    def _():
                        rs_copy(d, slot, u).wait_recv()
                        ring[d, slot, u] = (ring[d, slot, u].astype(F32) + part_sum[d, rows, :]).astype(BF16)

                    rs_copy(d, slot, u).start()

        return carry

    lax.fori_loop(0, NZ - 1, hop, 0)

    def fin_copy(cc):
        rows = pl.ds(pl.multiple_of(cc * sz.state_rows, sz.state_rows), sz.state_rows)
        return pltpu.make_async_remote_copy(
            src_ref=totals.at[:, rows], dst_ref=mine_out, send_sem=fin_send, recv_sem=fin_recv,
            device_id=device(dc=1), device_id_type=MESH,
        )

    @pl.when(native)
    def _():
        for d in range(2):
            product(d, z_lo)
        for d in range(2):
            for u in range(2):
                rows = slice(u * sub, (u + 1) * sub)
                rs_copy(d, z_lo, u).wait_recv()
                total = ring[d, z_lo, u].astype(F32) + part_sum[d, rows, :]
                totals[d, :, rows] = total.T.astype(BF16)
        fin_copy(1 - core).start()
        own = pl.ds(pl.multiple_of(core * sz.state_rows, sz.state_rows), sz.state_rows)
        mine_out[...] = totals[:, own, :]

    @pl.when(jnp.logical_not(native))
    def _():
        fin_copy(0).wait_recv()

    gradient, sample_grad = mine_out[0].astype(F32), mine_out[1].astype(F32)
    moment_new = BETA_ONE * moment[...].astype(F32) + (1.0 - BETA_ONE) * gradient
    curvature_new = BETA_TWO * curvature[...].astype(F32) + (1.0 - BETA_TWO) * sample_grad * sample_grad
    moment_out[...] = moment_new.astype(BF16)
    curvature_out[...] = curvature_new.astype(BF16)
    update_out[...] = jnp.clip(moment_new / (RHO_SCALE * curvature_new), -1.0, 1.0).astype(BF16)

    for copy in sent:
        copy.wait_send()
    w_finish()

    def drain(k, carry):
        for d in range(2):
            to = owner(d, k)

            @pl.when(to // Z_LO == core)
            def _():
                for u in range(2):
                    rs_copy(d, to % Z_LO, u).wait_send()

        return carry

    lax.fori_loop(0, NZ - 1, drain, 0)

    @pl.when(native)
    def _():
        fin_copy(0).wait_send()


def plane_labels(input_ids, sampled_ids, columns):
    rep, shard = lax.axis_index("rep"), lax.axis_index("shard")
    z_lo, core, z_hi, place = rep // CORES, rep % CORES, shard // PLANE, shard % PLANE
    tokens = input_ids.shape[0]
    span = tokens // (NZ * CORES)
    group = tokens // (Z_LO * CORES)
    first_col = (core * PLANE + place) * columns
    position = jnp.arange(tokens)
    targets = jnp.where(position % group < group - 1, jnp.roll(input_ids, -1), -1)

    def of_plane(ids):
        mine = ids.reshape(Z_LO, CORES, Z_HI, span)
        mine = lax.dynamic_slice(mine, (z_lo, 0, z_hi, 0), (1, CORES, 1, span))
        mine = mine.reshape(CORES, NX, NY, 2, -1)
        first = mine[:, :, :, 0].transpose(2, 1, 0, 3)
        second = mine[:, :, :, 1].transpose(1, 2, 0, 3)
        return jnp.concatenate([first, second]).reshape(TILES, -1)

    return of_plane(targets) - first_col, of_plane(sampled_ids) - first_col


def on_device(hidden, norm_gain, input_ids, sampled_ids, head_weight, moment, curvature):
    rows, features = hidden.shape
    columns = head_weight.shape[1]
    sz = Sizes(rows, features, columns, moment.shape[0])
    tgt, smp = plane_labels(input_ids, sampled_ids, columns)
    vmem = pl.BlockSpec(memory_space=pltpu.VMEM)
    state = jax.ShapeDtypeStruct(moment.shape, BF16)
    dma = pltpu.SemaphoreType.DMA
    n_chunks = sz.weight_chunks // 2
    return pl.pallas_call(
        lambda *refs: kernel(sz, *refs),
        out_shape=(state, state, state),
        in_specs=[vmem, vmem, vmem, vmem, pl.BlockSpec(memory_space=pl.ANY), vmem, vmem],
        out_specs=(vmem, vmem, vmem),
        scratch_shapes=[
            pltpu.VMEM((sz.tokens, features), BF16),
            pltpu.VMEM((features, columns), BF16),
            pltpu.VMEM((columns, features), BF16),
            pltpu.VMEM((TILES, columns, sz.tile), F32),
            pltpu.VMEM((2, columns, sz.tokens), BF16),
            pltpu.VMEM((2, Z_LO, 2, columns // 2, sz.quarter), BF16),
            pltpu.VMEM((2, columns, sz.quarter), F32),
            pltpu.VMEM((2, sz.quarter, columns), BF16),
            pltpu.VMEM((2, sz.state_rows, columns), BF16),
            pltpu.VMEM((2 * TILES, sz.tile), F32),
            pltpu.VMEM((7, 2 * TILES, sz.tile), F32),
            pltpu.VMEM((2 * TILES, sz.tile), F32),
            pltpu.VMEM((3, 2 * TILES, sz.tile), F32),
            pltpu.VMEM((TILES, sz.tile), F32),
            dma((2, 20)),
            dma((2, 4, 4, 2)),
            dma((2, 16)),
            dma((2, 16)),
            dma((2, n_chunks)),
            dma((2, n_chunks)),
            dma,
            dma((7,)),
            dma((7,)),
            dma((3,)),
            dma((3,)),
            dma((2, Z_LO, 2)),
            dma((2, Z_LO, 2)),
            dma,
            dma,
        ],
        compiler_params=pltpu.CompilerParams(
            collective_id=0, has_side_effects=True, vmem_limit_bytes=60 * 1024 * 1024
        ),
    )(hidden, norm_gain.reshape(1, -1), tgt, smp, head_weight, moment, curvature)


def solution(mesh):
    in_specs = (
        P(("rep", "shard"), None),
        P(),
        P(),
        P(),
        P(None, "shard"),
        P("rep", "shard"),
        P("rep", "shard"),
    )
    out_specs = (P("rep", "shard"), P("rep", "shard"), P("rep", "shard"))
    return jax.shard_map(
        on_device, mesh=mesh, in_specs=in_specs, out_specs=out_specs, check_vma=False
    )
```

```python
import jax
import jax.numpy as jnp
from jax import lax
from jax.experimental import pallas as pl
from jax.experimental.pallas import tpu as pltpu
from jax.sharding import PartitionSpec as P

EPS_NORM = 1e-05
BETA_ONE = 0.96
BETA_TWO = 0.95
RHO_SCALE = 0.05

NX = NY = 4
Z_LO, Z_HI, CORES = 4, 2, 2
NZ = Z_HI * Z_LO
PLANE = NX * NY
W_SLACK = 3
W_AHEAD = 4
RING_PARTS = 4
TILES = 2 * 4
BF16, F32 = jnp.bfloat16, jnp.float32
MESH = pl.DeviceIdType.MESH


class Sizes:
    def __init__(self, rows, features, columns, state_rows):
        self.rows = rows
        self.half = rows // 2
        self.part = rows // 4
        self.features = features
        self.columns = columns
        self.share = columns // CORES
        self.tile = 4 * CORES * self.half
        self.tokens = TILES * self.tile
        self.state_rows = state_rows
        self.quarter = CORES * state_rows
        self.weight_chunks = 32


def kernel(
    sz, hidden, gain, tgt, smp, weight, mine_out,
    normed, w_buf, w_t, expd, probs, ring, part_sum, totals, other,
    st_own, st_one, st_mid, st_two, factor,
    ag_send, ag_recv, sib_send, sib_recv, w_send, w_recv, w_local, s1_send, s1_recv, s2_send, s2_recv,
    rs_send, rs_recv, fin_send, fin_recv,
):
    rep, shard = lax.axis_index("rep"), lax.axis_index("shard")
    z_lo, core = rep // CORES, rep % CORES
    z_hi, x, y = shard // PLANE, (shard // NY) % NX, shard % NY
    z = z_hi * Z_LO + z_lo

    def device(dx=0, dy=0, dz=0, dc=0):
        xx, yy, zz, cc = (x + dx) % NX, (y + dy) % NY, (z + dz) % NZ, (core + dc) % CORES
        return ((zz % Z_LO) * CORES + cc, (zz // Z_LO) * PLANE + xx * NY + yy)

    row_peers = [(dx, dc) for dx in range(NX) for dc in range(CORES) if (dx, dc) != (0, 0)]
    column_peers = [1, 2, 3]
    barrier = pltpu.get_barrier_semaphore()
    partners = [device(dx=dx, dc=dc) for dx, dc in row_peers]
    partners += [device(dy=dy) for dy in column_peers]
    partners += [device(dz=1), device(dz=NZ - 1)]
    for partner in partners:
        pl.semaphore_signal(barrier, inc=1, device_id=partner, device_id_type=MESH)

    def block_row(h, da, db, cc):
        a, b = (x, y) if h == 0 else (y, x)
        return ((h * 4 + (b + db) % 4) * 4 + (a + da) % 4) * (CORES * sz.half) + cc * sz.half

    share = pl.ds(pl.multiple_of(core * sz.share, sz.share), sz.share)
    w_copy = pltpu.make_async_copy(weight.at[:, share], w_buf.at[z_hi], w_local)
    w_copy.start()

    for h in range(2):
        values = hidden[pl.ds(h * sz.half, sz.half), :].astype(F32)
        scale = lax.rsqrt(jnp.mean(values * values, axis=-1, keepdims=True) + EPS_NORM)
        rows = pl.ds(pl.multiple_of(block_row(h, 0, 0, core), sz.half), sz.half)
        normed[rows, :] = (values * scale * gain[...]).astype(BF16)
    pl.semaphore_wait(barrier, len(partners))

    sent = []

    def start(copy):
        copy.start()
        sent.append(copy)

    def ag_copy(h, da, db, part, along, step, index):
        to_a, to_b = (step, 0) if along == 0 else (0, step)
        dx, dy = (to_a, to_b) if h == 0 else (to_b, to_a)
        first = block_row(h, da, db, core)
        if part is None:
            rows = pl.ds(pl.multiple_of(first, sz.half), sz.half)
        else:
            rows = pl.ds(pl.multiple_of(first + part * sz.part, sz.part), sz.part)
        block = normed.at[rows]
        return pltpu.make_async_remote_copy(
            src_ref=block, dst_ref=block, send_sem=ag_send.at[h, index],
            recv_sem=ag_recv.at[h, (da - to_a) % 4, (db - to_b) % 4, part or 0],
            device_id=device(dx=dx, dy=dy), device_id_type=MESH,
        )

    counts = [0, 0]

    def ag_send_block(h, da, db, part, along, step):
        start(ag_copy(h, da % 4, db % 4, part, along, step, counts[h]))
        counts[h] += 1

    def ag_wait(h, da, db):
        da, db = da % 4, db % 4
        first = block_row(h, da, db, core)
        split = da == 2 if db == 0 else db == 2
        for part in (0, 1) if split else (None,):
            if part is None:
                rows = pl.ds(pl.multiple_of(first, sz.half), sz.half)
            else:
                rows = pl.ds(pl.multiple_of(first + part * sz.part, sz.part), sz.part)
            pltpu.make_async_remote_copy(
                src_ref=normed.at[rows], dst_ref=normed.at[rows], send_sem=ag_send.at[h, 0],
                recv_sem=ag_recv.at[h, da, db, part or 0], device_id=device(dx=1), device_id_type=MESH,
            ).wait_recv()

    def sib_copy(h, da, db, cc):
        rows = pl.ds(pl.multiple_of(block_row(h, da, db, cc), sz.half), sz.half)
        return pltpu.make_async_remote_copy(
            src_ref=normed.at[rows], dst_ref=normed.at[rows], send_sem=sib_send.at[h, (da % 4) * 4 + db % 4],
            recv_sem=sib_recv.at[h, (da % 4) * 4 + db % 4], device_id=device(dc=1), device_id_type=MESH,
        )

    def to_sibling(h, da, db):
        start(sib_copy(h, da, db, core))

    chunk = sz.features // sz.weight_chunks
    up_chunks = sz.weight_chunks // 2

    def w_copy_of(way, j, half):
        rows = pl.ds(pl.multiple_of((way * up_chunks + j) * chunk, chunk), chunk)
        block = w_buf.at[half, rows]
        return pltpu.make_async_remote_copy(
            src_ref=block, dst_ref=block, send_sem=w_send.at[way, j], recv_sem=w_recv.at[way, j],
            device_id=device(dz=1 if way == 0 else NZ - 1), device_id_type=MESH,
        )

    ends = [Z_LO - 1, 0]

    def w_first():
        for way in range(2):

            @pl.when(z_lo == ends[way])
            def _():
                for j in range(W_AHEAD):
                    w_copy_of(way, j, z_hi).start()

    def w_step(beat):
        for way in range(2):
            j = beat - W_SLACK * (z_lo if way == 0 else Z_LO - 1 - z_lo)

            @pl.when((j >= 0) & (j < up_chunks))
            def _():
                w_copy_of(way, j, 1 - z_hi).wait_recv()

                @pl.when(z_lo != ends[way])
                def _():
                    w_copy_of(way, j, 1 - z_hi).start()

            if beat + W_AHEAD < up_chunks:

                @pl.when(z_lo == ends[way])
                def _():
                    w_copy_of(way, beat, z_hi).wait_send()
                    w_copy_of(way, beat + W_AHEAD, z_hi).start()

    def w_finish():
        for way in range(2):
            for j in range(up_chunks):
                if j < up_chunks - W_AHEAD:

                    @pl.when(z_lo != ends[way])
                    def _():
                        w_copy_of(way, j, z_hi).wait_send()
                else:
                    w_copy_of(way, j, z_hi).wait_send()

    def logits_tile(t):
        rows = pl.ds(pl.multiple_of(t * sz.tile, sz.tile), sz.tile)
        logits = lax.dot_general(
            w_t[...], normed[rows, :], (((1,), (1,)), ((), ())), preferred_element_type=F32
        )
        peak = jnp.max(logits, axis=0, keepdims=True)
        scaled = jnp.exp(logits - peak)
        expd[t] = scaled
        st_own[pl.ds(t, 1), :] = peak
        st_own[pl.ds(TILES + t, 1), :] = jnp.sum(scaled, axis=0, keepdims=True)

    def two_tiles(offset):
        for h in range(2):
            for da in range(4):
                sib_copy(h, da, offset, core).wait_recv()

        def body(h, carry):
            logits_tile(h * 4 + jnp.where(h == 0, y + offset, x + offset) % 4)
            return carry

        lax.fori_loop(0, 2, body, 0)

    for h in range(2):
        for step in (1, -1):
            ag_send_block(h, 0, 0, None, 0, step)

    w_copy.wait()
    w_first()
    for h in range(2):
        for step in (1, -1):
            ag_send_block(h, 0, 0, None, 1, step)
        to_sibling(h, 0, 0)

    def forward_a(h):
        for da in (-1, 1):
            ag_wait(h, da, 0)
            ag_send_block(h, da, 0, 0 if da == -1 else 1, 0, -da)
        for da in (-1, 1):
            for step in (1, -1):
                ag_send_block(h, da, 0, None, 1, step)
            to_sibling(h, da, 0)

    def across_a(h):
        ag_wait(h, 2, 0)
        for step in (1, -1):
            ag_send_block(h, 2, 0, None, 1, step)
        to_sibling(h, 2, 0)

    def forward_b(h, da):
        for db in (-1, 1):
            ag_wait(h, da, db)
            ag_send_block(h, da, db, 0 if db == -1 else 1, 1, -db)
            to_sibling(h, da, db)

    def across_b(h, da):
        ag_wait(h, da, 2)
        to_sibling(h, da, 2)

    beats = iter(range(up_chunks + W_SLACK * (Z_LO - 1)))

    def w_beats(many):
        for _ in range(many):
            w_step(next(beats))

    w_beats(3)
    for h in range(2):
        forward_a(h)
    w_beats(4)
    for h in range(2):
        forward_b(h, 0)
    for h in range(2):
        across_a(h)
    w_beats(6)
    for h in range(2):
        forward_b(h, -1)
    w_beats(2)
    for h in range(2):
        forward_b(h, 1)
    w_beats(3)
    for h in range(2):
        across_b(h, 0)
    w_beats(5)
    for h in range(2):
        forward_b(h, 2)
    w_beats(2)

    slab = sz.columns

    def turn(j, carry):
        first = pl.multiple_of(j * slab, slab)
        for half in range(Z_HI):
            w_t[half * sz.share : (half + 1) * sz.share, pl.ds(first, slab)] = w_buf[half, pl.ds(first, slab), :].T
        return carry

    lax.fori_loop(0, sz.features // slab, turn, 0)
    two_tiles(0)
    two_tiles(1)
    for h in range(2):
        across_b(h, -1)
        across_b(h, 1)
    two_tiles(-1)
    for h in range(2):
        across_b(h, 2)
    two_tiles(2)

    def join(pairs):
        peak = pairs[0][0]
        for other, _ in pairs[1:]:
            peak = jnp.maximum(peak, other)
        total = 0.0
        for other, part in pairs:
            total = total + part * jnp.exp(other - peak)
        return peak, total

    def pair(ref):
        return ref[:TILES, :], ref[TILES:, :]

    ones = [
        pltpu.make_async_remote_copy(
            src_ref=st_own, dst_ref=st_one.at[j], send_sem=s1_send.at[j], recv_sem=s1_recv.at[j],
            device_id=device(dx=dx, dc=dc), device_id_type=MESH,
        )
        for j, (dx, dc) in enumerate(row_peers)
    ]
    for copy in ones:
        start(copy)
    for copy in ones:
        copy.wait_recv()
    peak, total = join([pair(st_own)] + [pair(st_one.at[j]) for j in range(len(row_peers))])
    st_mid[:TILES, :] = peak
    st_mid[TILES:, :] = total
    twos = [
        pltpu.make_async_remote_copy(
            src_ref=st_mid, dst_ref=st_two.at[j], send_sem=s2_send.at[j], recv_sem=s2_recv.at[j],
            device_id=device(dy=dy), device_id_type=MESH,
        )
        for j, dy in enumerate(column_peers)
    ]
    for copy in twos:
        start(copy)
    for copy in twos:
        copy.wait_recv()
    peak, total = join([pair(st_mid)] + [pair(st_two.at[j]) for j in range(len(column_peers))])
    factor[...] = jnp.exp(st_own[:TILES, :] - peak) / total

    def probs_tile(t, carry):
        scaled = expd[t] * factor[pl.ds(t, 1), :]
        row = lax.broadcasted_iota(jnp.int32, (Z_HI * sz.share, sz.tile), 0)
        column = jnp.where(row < sz.share, row, row + PLANE * sz.columns - sz.share)
        lanes = pl.ds(pl.multiple_of(t * sz.tile, sz.tile), sz.tile)
        for d, labels in enumerate((tgt, smp)):
            hit = column == labels[pl.ds(t, 1), :]
            probs[d, :, lanes] = jnp.where(hit, scaled - 1.0, scaled).astype(BF16)
        return carry

    lax.fori_loop(0, TILES, probs_tile, 0)

    sub = sz.share // RING_PARTS

    def rs_copy(d, slot, u):
        block = ring.at[d, slot, u]
        return pltpu.make_async_remote_copy(
            src_ref=block, dst_ref=block, send_sem=rs_send.at[d, slot, u], recv_sem=rs_recv.at[d, slot, u],
            device_id=device(dz=1 if d == 0 else NZ - 1), device_id_type=MESH,
        )

    def owner(d, k):
        return (z + NZ - 1 - k) % NZ if d == 0 else (z + 1 + k) % NZ

    def product(d, k):
        to = owner(d, k)
        rows = pl.ds(pl.multiple_of(to // Z_LO * sz.share, sz.share), sz.share)
        lanes = pl.ds(pl.multiple_of(to % Z_LO * sz.quarter, sz.quarter), sz.quarter)
        part_sum[k % 2, d] = jnp.dot(probs[d, rows, :], normed[:, lanes], preferred_element_type=F32)

    def piece(d, k, u):
        rows = slice(u * sub, (u + 1) * sub)
        slot = owner(d, k)

        @pl.when(k == 0)
        def _():
            ring[d, slot, u] = part_sum[k % 2, d, rows, :].astype(BF16)

        @pl.when(k > 0)
        def _():
            rs_copy(d, slot, u).wait_recv()
            ring[d, slot, u] = (ring[d, slot, u].astype(F32) + part_sum[k % 2, d, rows, :]).astype(BF16)

        rs_copy(d, slot, u).start()

    for d in range(2):
        product(d, 0)

    def hop(k, carry):
        for u in range(RING_PARTS):
            for d in range(2):
                piece(d, k, u)
            if u < 2:
                product(u, k + 1)
        return carry

    lax.fori_loop(0, NZ - 1, hop, 0)

    def fin_copy(d):
        rows = pl.ds(pl.multiple_of((1 - core) * sz.state_rows, sz.state_rows), sz.state_rows)
        return pltpu.make_async_remote_copy(
            src_ref=totals.at[d, rows], dst_ref=other.at[d], send_sem=fin_send.at[d], recv_sem=fin_recv.at[d],
            device_id=device(dc=1), device_id_type=MESH,
        )

    own = pl.ds(pl.multiple_of(core * sz.state_rows, sz.state_rows), sz.state_rows)
    for d in range(2):
        for first in range(0, sz.share, 128):
            rows = slice(first, first + 128)
            for u in range(first // sub, (first + 128) // sub):
                rs_copy(d, z, u).wait_recv()
            block = ring[d, z, first // sub : (first + 128) // sub].reshape(128, sz.quarter)
            total = block.astype(F32) + part_sum[(NZ - 1) % 2, d, rows, :]
            totals[d, :, rows] = total.T.astype(BF16)
        start(fin_copy(d))
        mine_out[d, :, share] = totals[d, own, :]
    others = pl.ds(pl.multiple_of((1 - core) * sz.share, sz.share), sz.share)
    for d in range(2):
        fin_copy(d).wait_recv()
        mine_out[d, :, others] = other[d]

    for copy in sent:
        copy.wait_send()
    w_finish()

    def drain(k, carry):
        for d in range(2):
            for u in range(RING_PARTS):
                rs_copy(d, owner(d, k), u).wait_send()
        return carry

    lax.fori_loop(0, NZ - 1, drain, 0)


def plane_labels(input_ids, sampled_ids, columns):
    rep, shard = lax.axis_index("rep"), lax.axis_index("shard")
    z_lo, core, z_hi, place = rep // CORES, rep % CORES, shard // PLANE, shard % PLANE
    tokens = input_ids.shape[0]
    span = tokens // (NZ * CORES)
    group = tokens // (Z_LO * CORES)
    first_col = place * columns + core * (columns // CORES)
    position = jnp.arange(tokens)
    targets = jnp.where(position % group < group - 1, jnp.roll(input_ids, -1), -1)

    def of_plane(ids):
        mine = ids.reshape(Z_LO, CORES, Z_HI, span)
        mine = lax.dynamic_slice(mine, (z_lo, 0, z_hi, 0), (1, CORES, 1, span))
        mine = mine.reshape(CORES, NX, NY, 2, -1)
        first = mine[:, :, :, 0].transpose(2, 1, 0, 3)
        second = mine[:, :, :, 1].transpose(1, 2, 0, 3)
        return jnp.concatenate([first, second]).reshape(TILES, -1)

    return of_plane(targets) - first_col, of_plane(sampled_ids) - first_col


def on_device(hidden, norm_gain, input_ids, sampled_ids, head_weight, moment, curvature):
    rows, features = hidden.shape
    columns = head_weight.shape[1]
    sz = Sizes(rows, features, columns, moment.shape[0])
    tgt, smp = plane_labels(input_ids, sampled_ids, columns)
    vmem = pl.BlockSpec(memory_space=pltpu.VMEM)
    dma = pltpu.SemaphoreType.DMA
    n_chunks = sz.weight_chunks // 2
    sums = pl.pallas_call(
        lambda *refs: kernel(sz, *refs),
        out_shape=jax.ShapeDtypeStruct((2, *moment.shape), BF16),
        in_specs=[vmem, vmem, vmem, vmem, pl.BlockSpec(memory_space=pl.ANY)],
        out_specs=vmem,
        scratch_shapes=[
            pltpu.VMEM((sz.tokens, features), BF16),
            pltpu.VMEM((Z_HI, features, sz.share), BF16),
            pltpu.VMEM((columns, features), BF16),
            pltpu.VMEM((TILES, columns, sz.tile), F32),
            pltpu.VMEM((2, columns, sz.tokens), BF16),
            pltpu.VMEM((2, NZ, RING_PARTS, sz.share // RING_PARTS, sz.quarter), BF16),
            pltpu.VMEM((2, 2, sz.share, sz.quarter), F32),
            pltpu.VMEM((2, sz.quarter, sz.share), BF16),
            pltpu.VMEM((2, sz.state_rows, sz.share), BF16),
            pltpu.VMEM((2 * TILES, sz.tile), F32),
            pltpu.VMEM((7, 2 * TILES, sz.tile), F32),
            pltpu.VMEM((2 * TILES, sz.tile), F32),
            pltpu.VMEM((3, 2 * TILES, sz.tile), F32),
            pltpu.VMEM((TILES, sz.tile), F32),
            dma((2, 20)),
            dma((2, 4, 4, 2)),
            dma((2, 16)),
            dma((2, 16)),
            dma((2, n_chunks)),
            dma((2, n_chunks)),
            dma,
            dma((7,)),
            dma((7,)),
            dma((3,)),
            dma((3,)),
            dma((2, NZ, RING_PARTS)),
            dma((2, NZ, RING_PARTS)),
            dma((2,)),
            dma((2,)),
        ],
        compiler_params=pltpu.CompilerParams(
            collective_id=0, has_side_effects=True, vmem_limit_bytes=60 * 1024 * 1024
        ),
    )(hidden, norm_gain.reshape(1, -1), tgt, smp, head_weight)
    gradient, sample_grad = sums[0].astype(F32), sums[1].astype(F32)
    moment_new = BETA_ONE * moment.astype(F32) + (1.0 - BETA_ONE) * gradient
    curvature_new = BETA_TWO * curvature.astype(F32) + (1.0 - BETA_TWO) * sample_grad * sample_grad
    update_direction = jnp.clip(moment_new / (RHO_SCALE * curvature_new), -1.0, 1.0)
    return moment_new.astype(BF16), curvature_new.astype(BF16), update_direction.astype(BF16)


def solution(mesh):
    in_specs = (
        P(("rep", "shard"), None),
        P(),
        P(),
        P(),
        P(None, "shard"),
        P("rep", "shard"),
        P("rep", "shard"),
    )
    out_specs = (P("rep", "shard"), P("rep", "shard"), P("rep", "shard"))
    return jax.shard_map(
        on_device, mesh=mesh, in_specs=in_specs, out_specs=out_specs, check_vma=False
    )
```

```python
import jax
import jax.numpy as jnp
from jax import lax
from jax.experimental import pallas as pl
from jax.experimental.pallas import tpu as pltpu
from jax.sharding import PartitionSpec as P

EPS_NORM = 1e-05
BETA_ONE = 0.96
BETA_TWO = 0.95
RHO_SCALE = 0.05

NX = NY = 4
Z_LO, Z_HI, CORES = 4, 2, 2
NZ = Z_HI * Z_LO
PLANE = NX * NY
W_SLACK = 2
W_AHEAD = 4
RING_PARTS = 4
TILES = 2 * 4
BF16, F32 = jnp.bfloat16, jnp.float32
MESH = pl.DeviceIdType.MESH


class Sizes:
    def __init__(self, rows, features, columns, state_rows):
        self.rows = rows
        self.half = rows // 2
        self.part = rows // 4
        self.features = features
        self.columns = columns
        self.share = columns // CORES
        self.tile = 4 * CORES * self.half
        self.tokens = TILES * self.tile
        self.state_rows = state_rows
        self.quarter = CORES * state_rows
        self.weight_chunks = 16


def kernel(
    sz, hidden, gain, input_ids, sampled_ids, weight, mine_out,
    normed, w_buf, w_t, expd, probs, ring, part_sum, totals, other,
    st_own, st_one, st_mid, st_two, factor, labels,
    ag_send, ag_recv, sib_send, sib_recv, w_send, w_recv, w_local, s1_send, s1_recv, s2_send, s2_recv,
    rs_send, rs_recv, fin_send, fin_recv,
):
    rep, shard = lax.axis_index("rep"), lax.axis_index("shard")
    z_lo, core = rep // CORES, rep % CORES
    z_hi, x, y = shard // PLANE, (shard // NY) % NX, shard % NY
    z = z_hi * Z_LO + z_lo

    def device(dx=0, dy=0, dz=0, dc=0):
        xx, yy, zz, cc = (x + dx) % NX, (y + dy) % NY, (z + dz) % NZ, (core + dc) % CORES
        return ((zz % Z_LO) * CORES + cc, (zz // Z_LO) * PLANE + xx * NY + yy)

    row_peers = [(dx, dc) for dx in range(NX) for dc in range(CORES) if (dx, dc) != (0, 0)]
    column_peers = [1, 2, 3]
    barrier = pltpu.get_barrier_semaphore()
    partners = [device(dx=dx, dc=dc) for dx, dc in row_peers]
    partners += [device(dy=dy) for dy in column_peers]
    partners += [device(dz=1), device(dz=NZ - 1)]
    for partner in partners:
        pl.semaphore_signal(barrier, inc=1, device_id=partner, device_id_type=MESH)

    def block_row(h, da, db, cc):
        a, b = (x, y) if h == 0 else (y, x)
        return ((h * 4 + (b + db) % 4) * 4 + (a + da) % 4) * (CORES * sz.half) + cc * sz.half

    share = pl.ds(pl.multiple_of(core * sz.share, sz.share), sz.share)
    w_copy = pltpu.make_async_copy(weight.at[:, share], w_buf.at[z_hi], w_local)
    w_copy.start()

    for h in range(2):
        values = hidden[pl.ds(h * sz.half, sz.half), :].astype(F32)
        scale = lax.rsqrt(jnp.mean(values * values, axis=-1, keepdims=True) + EPS_NORM)
        rows = pl.ds(pl.multiple_of(block_row(h, 0, 0, core), sz.half), sz.half)
        normed[rows, :] = (values * scale * gain[...]).astype(BF16)
    pl.semaphore_wait(barrier, len(partners))

    sent = []

    def start(copy):
        copy.start()
        sent.append(copy)

    def ag_copy(h, da, db, part, along, step, index):
        to_a, to_b = (step, 0) if along == 0 else (0, step)
        dx, dy = (to_a, to_b) if h == 0 else (to_b, to_a)
        first = block_row(h, da, db, core)
        if part is None:
            rows = pl.ds(pl.multiple_of(first, sz.half), sz.half)
        else:
            rows = pl.ds(pl.multiple_of(first + part * sz.part, sz.part), sz.part)
        block = normed.at[rows]
        return pltpu.make_async_remote_copy(
            src_ref=block, dst_ref=block, send_sem=ag_send.at[h, index],
            recv_sem=ag_recv.at[h, (da - to_a) % 4, (db - to_b) % 4, part or 0],
            device_id=device(dx=dx, dy=dy), device_id_type=MESH,
        )

    counts = [0, 0]

    def ag_send_block(h, da, db, part, along, step):
        start(ag_copy(h, da % 4, db % 4, part, along, step, counts[h]))
        counts[h] += 1

    def ag_wait(h, da, db):
        da, db = da % 4, db % 4
        first = block_row(h, da, db, core)
        split = da == 2 if db == 0 else db == 2
        for part in (0, 1) if split else (None,):
            if part is None:
                rows = pl.ds(pl.multiple_of(first, sz.half), sz.half)
            else:
                rows = pl.ds(pl.multiple_of(first + part * sz.part, sz.part), sz.part)
            pltpu.make_async_remote_copy(
                src_ref=normed.at[rows], dst_ref=normed.at[rows], send_sem=ag_send.at[h, 0],
                recv_sem=ag_recv.at[h, da, db, part or 0], device_id=device(dx=1), device_id_type=MESH,
            ).wait_recv()

    def sib_copy(h, da, db, cc):
        rows = pl.ds(pl.multiple_of(block_row(h, da, db, cc), sz.half), sz.half)
        return pltpu.make_async_remote_copy(
            src_ref=normed.at[rows], dst_ref=normed.at[rows], send_sem=sib_send.at[h, (da % 4) * 4 + db % 4],
            recv_sem=sib_recv.at[h, (da % 4) * 4 + db % 4], device_id=device(dc=1), device_id_type=MESH,
        )

    def to_sibling(h, da, db):
        start(sib_copy(h, da, db, core))

    chunk = sz.features // sz.weight_chunks
    up_chunks = sz.weight_chunks // 2

    def w_copy_of(way, j, half):
        rows = pl.ds(pl.multiple_of((way * up_chunks + j) * chunk, chunk), chunk)
        block = w_buf.at[half, rows]
        return pltpu.make_async_remote_copy(
            src_ref=block, dst_ref=block, send_sem=w_send.at[way, j], recv_sem=w_recv.at[way, j],
            device_id=device(dz=1 if way == 0 else NZ - 1), device_id_type=MESH,
        )

    ends = [Z_LO - 1, 0]

    def w_first():
        for way in range(2):

            @pl.when(z_lo == ends[way])
            def _():
                for j in range(W_AHEAD):
                    w_copy_of(way, j, z_hi).start()

    def w_step(beat):
        for way in range(2):
            j = beat - W_SLACK * (z_lo if way == 0 else Z_LO - 1 - z_lo)

            @pl.when((j >= 0) & (j < up_chunks))
            def _():
                w_copy_of(way, j, 1 - z_hi).wait_recv()

                @pl.when(z_lo != ends[way])
                def _():
                    w_copy_of(way, j, 1 - z_hi).start()

            if beat + W_AHEAD < up_chunks:

                @pl.when(z_lo == ends[way])
                def _():
                    w_copy_of(way, beat, z_hi).wait_send()
                    w_copy_of(way, beat + W_AHEAD, z_hi).start()

    def w_finish():
        for way in range(2):
            for j in range(up_chunks):
                if j < up_chunks - W_AHEAD:

                    @pl.when(z_lo != ends[way])
                    def _():
                        w_copy_of(way, j, z_hi).wait_send()
                else:
                    w_copy_of(way, j, z_hi).wait_send()

    def find_labels():
        lanes = input_ids.shape[1]
        span = NX * NY * sz.rows // lanes
        first_col = (shard % PLANE) * sz.columns + core * sz.share
        row = lax.broadcasted_iota(jnp.int32, (span, lanes), 0)
        lane = lax.broadcasted_iota(jnp.int32, (span, lanes), 1)
        found = [[], []]
        for cc in range(CORES):
            block = (z_lo * CORES + cc) * Z_HI + z_hi
            now = pl.ds(pl.multiple_of(block * span, span), span)
            later = pl.ds(pl.multiple_of((block + 1) % (NZ * CORES) * span, span), span)
            ids = input_ids[now, :]
            up = jnp.concatenate([ids[1:], input_ids[later, :][:1]], axis=0)
            following = jnp.where(lane == lanes - 1, pltpu.roll(up, lanes - 1, 1), pltpu.roll(ids, lanes - 1, 1))
            last = (z_hi == Z_HI - 1) & (row == span - 1) & (lane == lanes - 1)
            found[0].append(jnp.where(last, -1, following) - first_col)
            found[1].append(sampled_ids[now, :] - first_col)
        for d in range(2):
            for h in range(2):
                for b in range(4):
                    pieces = []
                    for a in range(4):
                        xx, yy = (a, b) if h == 0 else (b, a)
                        at = (xx * NY + yy) * sz.rows + h * sz.half
                        for cc in range(CORES):
                            pieces.append(found[d][cc][at // lanes : at // lanes + 1, at % lanes : at % lanes + sz.half])
                    labels[d, h * 4 + b : h * 4 + b + 1, :] = jnp.concatenate(pieces, axis=1)

    def logits_tile(t):
        rows = pl.ds(pl.multiple_of(t * sz.tile, sz.tile), sz.tile)
        logits = lax.dot_general(
            w_t[...], normed[rows, :], (((1,), (1,)), ((), ())), preferred_element_type=F32
        )
        peak = jnp.max(logits, axis=0, keepdims=True)
        scaled = jnp.exp(logits - peak)
        expd[t] = scaled
        st_own[pl.ds(t, 1), :] = peak
        st_own[pl.ds(TILES + t, 1), :] = jnp.sum(scaled, axis=0, keepdims=True)

    def two_tiles(offset):
        for h in range(2):
            for da in range(4):
                sib_copy(h, da, offset, core).wait_recv()

        def body(h, carry):
            logits_tile(h * 4 + jnp.where(h == 0, y + offset, x + offset) % 4)
            return carry

        lax.fori_loop(0, 2, body, 0)

    for h in range(2):
        for step in (1, -1):
            ag_send_block(h, 0, 0, None, 0, step)

    w_copy.wait()
    w_first()
    for h in range(2):
        for step in (1, -1):
            ag_send_block(h, 0, 0, None, 1, step)
        to_sibling(h, 0, 0)

    def forward_a(h):
        for da in (-1, 1):
            ag_wait(h, da, 0)
            ag_send_block(h, da, 0, 0 if da == -1 else 1, 0, -da)
        for da in (-1, 1):
            for step in (1, -1):
                ag_send_block(h, da, 0, None, 1, step)
            to_sibling(h, da, 0)

    def across_a(h):
        ag_wait(h, 2, 0)
        for step in (1, -1):
            ag_send_block(h, 2, 0, None, 1, step)
        to_sibling(h, 2, 0)

    def forward_b(h, da):
        for db in (-1, 1):
            ag_wait(h, da, db)
            ag_send_block(h, da, db, 0 if db == -1 else 1, 1, -db)
            to_sibling(h, da, db)

    def across_b(h, da):
        ag_wait(h, da, 2)
        to_sibling(h, da, 2)

    beats = iter(range(up_chunks + W_SLACK * (Z_LO - 1)))

    def w_beats(many):
        for _ in range(many):
            w_step(next(beats))

    slab = sz.columns

    def turn(half):
        def body(j, carry):
            first = pl.multiple_of(j * slab, slab)
            rows = pl.ds(pl.multiple_of(half * sz.share, sz.share), sz.share)
            w_t[rows, pl.ds(first, slab)] = w_buf[half, pl.ds(first, slab), :].T
            return carry

        lax.fori_loop(0, sz.features // slab, body, 0)

    turn(z_hi)
    w_beats(3)
    for h in range(2):
        forward_a(h)
    find_labels()
    w_beats(4)
    for h in range(2):
        forward_b(h, 0)
    for h in range(2):
        across_a(h)
    w_beats(3)
    for h in range(2):
        forward_b(h, -1)
        forward_b(h, 1)
    for h in range(2):
        across_b(h, 0)
    w_beats(3)
    for h in range(2):
        forward_b(h, 2)
    w_beats(1)
    turn(1 - z_hi)
    two_tiles(0)
    two_tiles(1)
    for h in range(2):
        across_b(h, -1)
        across_b(h, 1)
    two_tiles(-1)
    for h in range(2):
        across_b(h, 2)
    two_tiles(2)

    def join(pairs):
        peak = pairs[0][0]
        for other, _ in pairs[1:]:
            peak = jnp.maximum(peak, other)
        total = 0.0
        for other, part in pairs:
            total = total + part * jnp.exp(other - peak)
        return peak, total

    def pair(ref):
        return ref[:TILES, :], ref[TILES:, :]

    ones = [
        pltpu.make_async_remote_copy(
            src_ref=st_own, dst_ref=st_one.at[j], send_sem=s1_send.at[j], recv_sem=s1_recv.at[j],
            device_id=device(dx=dx, dc=dc), device_id_type=MESH,
        )
        for j, (dx, dc) in enumerate(row_peers)
    ]
    for copy in ones:
        start(copy)
    for copy in ones:
        copy.wait_recv()
    peak, total = join([pair(st_own)] + [pair(st_one.at[j]) for j in range(len(row_peers))])
    st_mid[:TILES, :] = peak
    st_mid[TILES:, :] = total
    twos = [
        pltpu.make_async_remote_copy(
            src_ref=st_mid, dst_ref=st_two.at[j], send_sem=s2_send.at[j], recv_sem=s2_recv.at[j],
            device_id=device(dy=dy), device_id_type=MESH,
        )
        for j, dy in enumerate(column_peers)
    ]
    for copy in twos:
        start(copy)
    for copy in twos:
        copy.wait_recv()
    peak, total = join([pair(st_mid)] + [pair(st_two.at[j]) for j in range(len(column_peers))])
    factor[...] = jnp.exp(st_own[:TILES, :] - peak) / total

    def probs_tile(t, carry):
        scaled = expd[t] * factor[pl.ds(t, 1), :]
        row = lax.broadcasted_iota(jnp.int32, (Z_HI * sz.share, sz.tile), 0)
        column = jnp.where(row < sz.share, row, row + PLANE * sz.columns - sz.share)
        lanes = pl.ds(pl.multiple_of(t * sz.tile, sz.tile), sz.tile)
        for d in range(2):
            hit = column == labels[d, pl.ds(t, 1), :]
            probs[d, :, lanes] = jnp.where(hit, scaled - 1.0, scaled).astype(BF16)
        return carry

    lax.fori_loop(0, TILES, probs_tile, 0)

    sub = sz.share // RING_PARTS

    def rs_copy(d, slot, u):
        block = ring.at[d, slot, u]
        return pltpu.make_async_remote_copy(
            src_ref=block, dst_ref=block, send_sem=rs_send.at[d, slot, u], recv_sem=rs_recv.at[d, slot, u],
            device_id=device(dz=1 if d == 0 else NZ - 1), device_id_type=MESH,
        )

    def owner(d, k):
        return (z + NZ - 1 - k) % NZ if d == 0 else (z + 1 + k) % NZ

    def product(d, k):
        to = owner(d, k)
        rows = pl.ds(pl.multiple_of(to // Z_LO * sz.share, sz.share), sz.share)
        lanes = pl.ds(pl.multiple_of(to % Z_LO * sz.quarter, sz.quarter), sz.quarter)
        part_sum[k % 2, d] = jnp.dot(probs[d, rows, :], normed[:, lanes], preferred_element_type=F32)

    def piece(d, k, u):
        rows = slice(u * sub, (u + 1) * sub)
        slot = owner(d, k)

        @pl.when(k == 0)
        def _():
            ring[d, slot, u] = part_sum[k % 2, d, rows, :].astype(BF16)

        @pl.when(k > 0)
        def _():
            rs_copy(d, slot, u).wait_recv()
            ring[d, slot, u] = (ring[d, slot, u].astype(F32) + part_sum[k % 2, d, rows, :]).astype(BF16)

        rs_copy(d, slot, u).start()

    for d in range(2):
        product(d, 0)

    def hop(k, carry):
        for u in range(RING_PARTS):
            for d in range(2):
                piece(d, k, u)
            if u < 2:
                product(u, k + 1)
        return carry

    lax.fori_loop(0, NZ - 1, hop, 0)

    def fin_copy(d):
        rows = pl.ds(pl.multiple_of((1 - core) * sz.state_rows, sz.state_rows), sz.state_rows)
        return pltpu.make_async_remote_copy(
            src_ref=totals.at[d, rows], dst_ref=other.at[d], send_sem=fin_send.at[d], recv_sem=fin_recv.at[d],
            device_id=device(dc=1), device_id_type=MESH,
        )

    own = pl.ds(pl.multiple_of(core * sz.state_rows, sz.state_rows), sz.state_rows)
    for d in range(2):
        for first in range(0, sz.share, 128):
            rows = slice(first, first + 128)
            for u in range(first // sub, (first + 128) // sub):
                rs_copy(d, z, u).wait_recv()
            block = ring[d, z, first // sub : (first + 128) // sub].reshape(128, sz.quarter)
            total = block.astype(F32) + part_sum[(NZ - 1) % 2, d, rows, :]
            totals[d, :, rows] = total.T.astype(BF16)
        start(fin_copy(d))
        mine_out[d, :, share] = totals[d, own, :]
    others = pl.ds(pl.multiple_of((1 - core) * sz.share, sz.share), sz.share)
    for d in range(2):
        fin_copy(d).wait_recv()
        mine_out[d, :, others] = other[d]

    for copy in sent:
        copy.wait_send()
    w_finish()

    def drain(k, carry):
        for d in range(2):
            for u in range(RING_PARTS):
                rs_copy(d, owner(d, k), u).wait_send()
        return carry

    lax.fori_loop(0, NZ - 1, drain, 0)


def on_device(hidden, norm_gain, input_ids, sampled_ids, head_weight, moment, curvature):
    rows, features = hidden.shape
    columns = head_weight.shape[1]
    sz = Sizes(rows, features, columns, moment.shape[0])
    lanes = 128
    vmem = pl.BlockSpec(memory_space=pltpu.VMEM)
    dma = pltpu.SemaphoreType.DMA
    n_chunks = sz.weight_chunks // 2
    sums = pl.pallas_call(
        lambda *refs: kernel(sz, *refs),
        out_shape=jax.ShapeDtypeStruct((2, *moment.shape), BF16),
        in_specs=[vmem, vmem, vmem, vmem, pl.BlockSpec(memory_space=pl.ANY)],
        out_specs=vmem,
        scratch_shapes=[
            pltpu.VMEM((sz.tokens, features), BF16),
            pltpu.VMEM((Z_HI, features, sz.share), BF16),
            pltpu.VMEM((columns, features), BF16),
            pltpu.VMEM((TILES, columns, sz.tile), F32),
            pltpu.VMEM((2, columns, sz.tokens), BF16),
            pltpu.VMEM((2, NZ, RING_PARTS, sz.share // RING_PARTS, sz.quarter), BF16),
            pltpu.VMEM((2, 2, sz.share, sz.quarter), F32),
            pltpu.VMEM((2, sz.quarter, sz.share), BF16),
            pltpu.VMEM((2, sz.state_rows, sz.share), BF16),
            pltpu.VMEM((2 * TILES, sz.tile), F32),
            pltpu.VMEM((7, 2 * TILES, sz.tile), F32),
            pltpu.VMEM((2 * TILES, sz.tile), F32),
            pltpu.VMEM((3, 2 * TILES, sz.tile), F32),
            pltpu.VMEM((TILES, sz.tile), F32),
            pltpu.VMEM((2, TILES, sz.tile), jnp.int32),
            dma((2, 20)),
            dma((2, 4, 4, 2)),
            dma((2, 16)),
            dma((2, 16)),
            dma((2, n_chunks)),
            dma((2, n_chunks)),
            dma,
            dma((7,)),
            dma((7,)),
            dma((3,)),
            dma((3,)),
            dma((2, NZ, RING_PARTS)),
            dma((2, NZ, RING_PARTS)),
            dma((2,)),
            dma((2,)),
        ],
        compiler_params=pltpu.CompilerParams(
            collective_id=0, has_side_effects=True, vmem_limit_bytes=60 * 1024 * 1024
        ),
    )(hidden, norm_gain.reshape(1, -1), input_ids.reshape(-1, lanes), sampled_ids.reshape(-1, lanes), head_weight)
    gradient, sample_grad = sums[0].astype(F32), sums[1].astype(F32)
    moment_new = BETA_ONE * moment.astype(F32) + (1.0 - BETA_ONE) * gradient
    curvature_new = BETA_TWO * curvature.astype(F32) + (1.0 - BETA_TWO) * sample_grad * sample_grad
    update_direction = jnp.clip(moment_new / (RHO_SCALE * curvature_new), -1.0, 1.0)
    return moment_new.astype(BF16), curvature_new.astype(BF16), update_direction.astype(BF16)


def solution(mesh):
    in_specs = (
        P(("rep", "shard"), None),
        P(),
        P(),
        P(),
        P(None, "shard"),
        P("rep", "shard"),
        P("rep", "shard"),
    )
    out_specs = (P("rep", "shard"), P("rep", "shard"), P("rep", "shard"))
    return jax.shard_map(
        on_device, mesh=mesh, in_specs=in_specs, out_specs=out_specs, check_vma=False
    )
```

```python
import jax
import jax.numpy as jnp
from jax import lax
from jax.experimental import pallas as pl
from jax.experimental.pallas import tpu as pltpu
from jax.sharding import PartitionSpec as P

EPS_NORM = 1e-05
BETA_ONE = 0.96
BETA_TWO = 0.95
RHO_SCALE = 0.05

NX = NY = 4
Z_LO, Z_HI, CORES = 4, 2, 2
NZ = Z_HI * Z_LO
PLANE = NX * NY
W_SLACK = 2
W_AHEAD = 4
RING_PARTS = 2
TILES = 2 * 4
BF16, F32 = jnp.bfloat16, jnp.float32
MESH = pl.DeviceIdType.MESH


class Sizes:
    def __init__(self, rows, features, columns, state_rows):
        self.rows = rows
        self.half = rows // 2
        self.part = rows // 4
        self.features = features
        self.columns = columns
        self.share = columns // CORES
        self.tile = 4 * CORES * self.half
        self.tokens = TILES * self.tile
        self.state_rows = state_rows
        self.quarter = CORES * state_rows
        self.weight_chunks = 16
        self.wide = 256
        self.middle = self.quarter - 2 * self.wide
        self.lanes = self.quarter + self.middle
        self.far_block = NZ // 2 * CORES * rows
        self.far_tokens = 2 * PLANE * self.far_block


def kernel(
    sz, hidden, gain, input_ids, sampled_ids, weight, mine_out,
    normed, w_buf, w_t, expd, probs, plain, ring, part_sum, totals, other, other_sample,
    own_rows, far, far_sum, far_turned, far_labels,
    st_own, st_one, st_mid, st_two, factor, labels,
    ag_send, ag_recv, sib_send, sib_recv, w_send, w_recv, w_local, s1_send, s1_recv, s2_send, s2_recv,
    rs_send, rs_recv, fin_send, fin_recv, x_send, x_recv, f_send, f_recv,
):
    rep, shard = lax.axis_index("rep"), lax.axis_index("shard")
    z_lo, core = rep // CORES, rep % CORES
    z_hi, x, y = shard // PLANE, (shard // NY) % NX, shard % NY
    z = z_hi * Z_LO + z_lo

    def device(dx=0, dy=0, dz=0, dc=0):
        xx, yy, zz, cc = (x + dx) % NX, (y + dy) % NY, (z + dz) % NZ, (core + dc) % CORES
        return ((zz % Z_LO) * CORES + cc, (zz // Z_LO) * PLANE + xx * NY + yy)

    row_peers = [(dx, dc) for dx in range(NX) for dc in range(CORES) if (dx, dc) != (0, 0)]
    column_peers = [1, 2, 3]
    barrier = pltpu.get_barrier_semaphore()
    partners = [device(dx=dx, dc=dc) for dx, dc in row_peers]
    partners += [device(dy=dy) for dy in column_peers]
    partners += [device(dz=dz, dc=dc) for dz in range(1, NZ) for dc in range(CORES)]
    for partner in partners:
        pl.semaphore_signal(barrier, inc=1, device_id=partner, device_id_type=MESH)

    def block_row(h, da, db, cc):
        a, b = (x, y) if h == 0 else (y, x)
        return ((h * 4 + (b + db) % 4) * 4 + (a + da) % 4) * (CORES * sz.half) + cc * sz.half

    share = pl.ds(pl.multiple_of(core * sz.share, sz.share), sz.share)
    w_copy = pltpu.make_async_copy(weight.at[:, share], w_buf.at[z_hi], w_local)
    w_copy.start()

    for h in range(2):
        values = hidden[pl.ds(h * sz.half, sz.half), :].astype(F32)
        scale = lax.rsqrt(jnp.mean(values * values, axis=-1, keepdims=True) + EPS_NORM)
        rows = pl.ds(pl.multiple_of(block_row(h, 0, 0, core), sz.half), sz.half)
        block = (values * scale * gain[...]).astype(BF16)
        normed[rows, :] = block
        own_rows[h * sz.half : (h + 1) * sz.half, :] = block
    far_sum[...] = jnp.zeros_like(far_sum)
    pl.semaphore_wait(barrier, len(partners))

    sent = []

    def start(copy):
        copy.start()
        sent.append(copy)

    class Gather:
        def __init__(self, buffer, first_row, size, send_sems, recv_sems, on_arrival):
            self.buffer, self.first_row, self.size = buffer, first_row, size
            self.send_sems, self.recv_sems, self.on_arrival = send_sems, recv_sems, on_arrival
            self.sends = []

        def block(self, h, da, db, part):
            first = self.first_row(h, da, db)
            if part is None:
                return self.buffer.at[pl.ds(pl.multiple_of(first, self.size), self.size)]
            size = self.size // 2
            return self.buffer.at[pl.ds(pl.multiple_of(first + part * size, size), size)]

        def copy(self, index, h, da, db, part, along, step):
            to_a, to_b = (step, 0) if along == 0 else (0, step)
            dx, dy = (to_a, to_b) if h == 0 else (to_b, to_a)
            block = self.block(h, da, db, part)
            return pltpu.make_async_remote_copy(
                src_ref=block, dst_ref=block, send_sem=self.send_sems.at[index],
                recv_sem=self.recv_sems.at[h, (da - to_a) % 4, (db - to_b) % 4, part or 0],
                device_id=device(dx=dx, dy=dy), device_id_type=MESH,
            )

        def send(self, *what):
            self.copy(len(self.sends), *what).start()
            self.sends.append(what)

        def wait_sends(self):
            for index, what in enumerate(self.sends):
                self.copy(index, *what).wait_send()

        def wait(self, h, da, db):
            split = da % 4 == 2 if db % 4 == 0 else db % 4 == 2
            for part in (0, 1) if split else (None,):
                block = self.block(h, da, db, part)
                pltpu.make_async_remote_copy(
                    src_ref=block, dst_ref=block, send_sem=self.send_sems.at[0],
                    recv_sem=self.recv_sems.at[h, da % 4, db % 4, part or 0],
                    device_id=device(dx=1), device_id_type=MESH,
                ).wait_recv()

        def begin(self, along):
            for h in range(2):
                for step in (1, -1):
                    self.send(h, 0, 0, None, along, step)

        def forward_a(self, h):
            for da in (-1, 1):
                self.wait(h, da, 0)
                self.send(h, da, 0, 0 if da == -1 else 1, 0, -da)
            for da in (-1, 1):
                for step in (1, -1):
                    self.send(h, da, 0, None, 1, step)
                self.on_arrival(h, da, 0)

        def across_a(self, h):
            self.wait(h, 2, 0)
            for step in (1, -1):
                self.send(h, 2, 0, None, 1, step)
            self.on_arrival(h, 2, 0)

        def forward_b(self, h, da):
            for db in (-1, 1):
                self.wait(h, da, db)
                self.send(h, da, db, 0 if db == -1 else 1, 1, -db)
                self.on_arrival(h, da, db)

        def across_b(self, h, da):
            self.wait(h, da, 2)
            self.on_arrival(h, da, 2)

    def sib_copy(h, da, db, cc):
        rows = pl.ds(pl.multiple_of(block_row(h, da, db, cc), sz.half), sz.half)
        return pltpu.make_async_remote_copy(
            src_ref=normed.at[rows], dst_ref=normed.at[rows], send_sem=sib_send.at[h, (da % 4) * 4 + db % 4],
            recv_sem=sib_recv.at[h, (da % 4) * 4 + db % 4], device_id=device(dc=1), device_id_type=MESH,
        )

    def to_sibling(h, da, db):
        start(sib_copy(h, da, db, core))

    chunk = sz.features // sz.weight_chunks
    up_chunks = sz.weight_chunks // 2

    def w_copy_of(way, j, half):
        rows = pl.ds(pl.multiple_of((way * up_chunks + j) * chunk, chunk), chunk)
        block = w_buf.at[half, rows]
        return pltpu.make_async_remote_copy(
            src_ref=block, dst_ref=block, send_sem=w_send.at[way, j], recv_sem=w_recv.at[way, j],
            device_id=device(dz=1 if way == 0 else NZ - 1), device_id_type=MESH,
        )

    ends = [Z_LO - 1, 0]

    def w_first():
        for way in range(2):

            @pl.when(z_lo == ends[way])
            def _():
                for j in range(W_AHEAD):
                    w_copy_of(way, j, z_hi).start()

    def w_step(beat):
        for way in range(2):
            j = beat - W_SLACK * (z_lo if way == 0 else Z_LO - 1 - z_lo)

            @pl.when((j >= 0) & (j < up_chunks))
            def _():
                w_copy_of(way, j, 1 - z_hi).wait_recv()

                @pl.when(z_lo != ends[way])
                def _():
                    w_copy_of(way, j, 1 - z_hi).start()

            if beat + W_AHEAD < up_chunks:

                @pl.when(z_lo == ends[way])
                def _():
                    w_copy_of(way, beat, z_hi).wait_send()
                    w_copy_of(way, beat + W_AHEAD, z_hi).start()

    def w_finish():
        for way in range(2):
            for j in range(up_chunks):
                if j < up_chunks - W_AHEAD:

                    @pl.when(z_lo != ends[way])
                    def _():
                        w_copy_of(way, j, z_hi).wait_send()
                else:
                    w_copy_of(way, j, z_hi).wait_send()

    def find_labels():
        lanes = input_ids.shape[1]
        span = NX * NY * sz.rows // lanes
        first_col = (shard % PLANE) * sz.columns + core * sz.share
        row = lax.broadcasted_iota(jnp.int32, (span, lanes), 0)
        lane = lax.broadcasted_iota(jnp.int32, (span, lanes), 1)
        found = [[], []]
        for cc in range(CORES):
            block = (z_lo * CORES + cc) * Z_HI + z_hi
            now = pl.ds(pl.multiple_of(block * span, span), span)
            later = pl.ds(pl.multiple_of((block + 1) % (NZ * CORES) * span, span), span)
            ids = input_ids[now, :]
            up = jnp.concatenate([ids[1:], input_ids[later, :][:1]], axis=0)
            following = jnp.where(lane == lanes - 1, pltpu.roll(up, lanes - 1, 1), pltpu.roll(ids, lanes - 1, 1))
            last = (z_hi == Z_HI - 1) & (row == span - 1) & (lane == lanes - 1)
            found[0].append(jnp.where(last, -1, following) - first_col)
            found[1].append(sampled_ids[now, :] - first_col)
        for d in range(2):
            for h in range(2):
                for b in range(4):
                    pieces = []
                    for a in range(4):
                        xx, yy = (a, b) if h == 0 else (b, a)
                        at = (xx * NY + yy) * sz.rows + h * sz.half
                        for cc in range(CORES):
                            pieces.append(found[d][cc][at // lanes : at // lanes + 1, at % lanes : at % lanes + sz.half])
                    labels[d, h * 4 + b : h * 4 + b + 1, :] = jnp.concatenate(pieces, axis=1)

    def logits_tile(t):
        rows = pl.ds(pl.multiple_of(t * sz.tile, sz.tile), sz.tile)
        logits = lax.dot_general(
            w_t[...], normed[rows, :], (((1,), (1,)), ((), ())), preferred_element_type=F32
        )
        peak = jnp.max(logits, axis=0, keepdims=True)
        scaled = jnp.exp(logits - peak)
        expd[t] = scaled
        st_own[pl.ds(t, 1), :] = peak
        st_own[pl.ds(TILES + t, 1), :] = jnp.sum(scaled, axis=0, keepdims=True)

    def two_tiles(offset):
        for h in range(2):
            for da in range(4):
                sib_copy(h, da, offset, core).wait_recv()

        def body(h, carry):
            logits_tile(h * 4 + jnp.where(h == 0, y + offset, x + offset) % 4)
            return carry

        lax.fori_loop(0, 2, body, 0)

    near = Gather(normed, lambda h, da, db: block_row(h, da, db, core), sz.half, ag_send, ag_recv, to_sibling)
    near.begin(0)
    w_copy.wait()
    w_first()
    near.begin(1)
    for h in range(2):
        to_sibling(h, 0, 0)

    beats = iter(range(up_chunks + W_SLACK * (Z_LO - 1)))

    def w_beats(many):
        for _ in range(many):
            w_step(next(beats))

    slab = sz.columns

    def turn(half):
        def body(j, carry):
            first = pl.multiple_of(j * slab, slab)
            rows = pl.ds(pl.multiple_of(half * sz.share, sz.share), sz.share)
            w_t[rows, pl.ds(first, slab)] = w_buf[half, pl.ds(first, slab), :].T
            return carry

        lax.fori_loop(0, sz.features // slab, body, 0)

    def far_row(h, da, db):
        a, b = (x, y) if h == 0 else (y, x)
        return ((h * 4 + (b + db) % 4) * 4 + (a + da) % 4) * sz.far_block

    def far_lanes(dz, dc):
        first = (z + dz) % NZ % Z_LO * sz.quarter + (core + dc) % CORES * (sz.quarter - sz.wide)
        return pl.ds(pl.multiple_of(first, 128), sz.wide)

    def far_own(zz, cc):
        place = jnp.where(zz // Z_LO == 0, y * 4 + x, x * 4 + y)
        first = (zz // Z_LO * PLANE + place) * sz.far_block + (zz % Z_LO * CORES + cc) * sz.rows
        return pl.ds(pl.multiple_of(first, sz.rows), sz.rows)

    offsets = [(dz, dc) for dz in range(NZ) for dc in range(CORES) if (dz, dc) != (0, 0)]

    def exchange(dz, dc):
        return pltpu.make_async_remote_copy(
            src_ref=own_rows.at[:, far_lanes(dz, dc)], dst_ref=far.at[far_own(z, core)],
            send_sem=x_send.at[dz, dc], recv_sem=x_recv.at[dz, dc],
            device_id=device(dz=dz, dc=dc), device_id_type=MESH,
        )

    def exchange_start():
        for dz, dc in offsets:
            start(exchange(dz, dc))
        far[far_own(z, core), :] = own_rows[:, far_lanes(0, 0)]

    def exchange_wait():
        for dz, dc in offsets:
            exchange(dz, dc).wait_recv()

    second = Gather(far, far_row, sz.far_block, f_send, f_recv, lambda h, da, db: None)

    def find_far_labels():
        lanes = input_ids.shape[1]
        rows = input_ids.shape[0]
        span = rows // (NZ * CORES)
        ids = input_ids[...]
        row = lax.broadcasted_iota(jnp.int32, (rows, lanes), 0)
        lane = lax.broadcasted_iota(jnp.int32, (rows, lanes), 1)
        up = jnp.concatenate([ids[1:], ids[:1]], axis=0)
        following = jnp.where(lane == lanes - 1, pltpu.roll(up, lanes - 1, 1), pltpu.roll(ids, lanes - 1, 1))
        last = (row % (Z_HI * span) == Z_HI * span - 1) & (lane == lanes - 1)
        for d, found in enumerate((jnp.where(last, -1, following), sampled_ids[...])):
            found = found - shard * sz.columns
            for h in range(Z_HI):
                for odd in range(2):
                    pieces = []
                    for rr in range(Z_LO * CORES):
                        first = (rr * Z_HI + h) * span
                        pieces.append(found[first : first + span, odd * sz.rows : (odd + 1) * sz.rows])
                    far_labels[d, h, odd] = jnp.concatenate(pieces, axis=1)

    def far_blocks(offset):
        def body(i, carry):
            h, a = i // 4, i % 4
            b = (jnp.where(h == 0, y, x) + offset) % 4
            rows = pl.ds(pl.multiple_of((i // 4 * PLANE + b * 4 + a) * sz.far_block, sz.far_block), sz.far_block)
            place = jnp.where(h == 0, a * 4 + b, b * 4 + a)
            column = lax.broadcasted_iota(jnp.int32, (sz.columns, sz.far_block), 0)
            for d in range(2):
                hit = column == far_labels[d, h, place % 2, pl.ds(place // 2, 1), :]
                one_hot = jnp.where(hit, 1.0, 0.0).astype(BF16)
                far_sum[d] += jnp.dot(one_hot, far[rows, :], preferred_element_type=F32)
            return carry

        lax.fori_loop(0, 8, body, 0)

    turn(z_hi)
    w_beats(3)
    for h in range(2):
        near.forward_a(h)
    find_labels()
    w_beats(4)
    for h in range(2):
        near.forward_b(h, 0)
    for h in range(2):
        near.across_a(h)
    w_beats(3)
    for h in range(2):
        near.forward_b(h, -1)
        near.forward_b(h, 1)
    for h in range(2):
        near.across_b(h, 0)
    w_beats(3)
    for h in range(2):
        near.forward_b(h, 2)
    w_beats(1)
    exchange_start()
    turn(1 - z_hi)
    two_tiles(0)
    two_tiles(1)
    for h in range(2):
        near.across_b(h, -1)
        near.across_b(h, 1)
    two_tiles(-1)
    for h in range(2):
        near.across_b(h, 2)
    two_tiles(2)

    def join(pairs):
        peak = pairs[0][0]
        for other, _ in pairs[1:]:
            peak = jnp.maximum(peak, other)
        total = 0.0
        for other, part in pairs:
            total = total + part * jnp.exp(other - peak)
        return peak, total

    def pair(ref):
        return ref[:TILES, :], ref[TILES:, :]

    ones = [
        pltpu.make_async_remote_copy(
            src_ref=st_own, dst_ref=st_one.at[j], send_sem=s1_send.at[j], recv_sem=s1_recv.at[j],
            device_id=device(dx=dx, dc=dc), device_id_type=MESH,
        )
        for j, (dx, dc) in enumerate(row_peers)
    ]
    for copy in ones:
        start(copy)
    for copy in ones:
        copy.wait_recv()
    peak, total = join([pair(st_own)] + [pair(st_one.at[j]) for j in range(len(row_peers))])
    st_mid[:TILES, :] = peak
    st_mid[TILES:, :] = total
    twos = [
        pltpu.make_async_remote_copy(
            src_ref=st_mid, dst_ref=st_two.at[j], send_sem=s2_send.at[j], recv_sem=s2_recv.at[j],
            device_id=device(dy=dy), device_id_type=MESH,
        )
        for j, dy in enumerate(column_peers)
    ]
    for copy in twos:
        start(copy)
    exchange_wait()
    second.begin(0)
    second.begin(1)
    for copy in twos:
        copy.wait_recv()
    peak, total = join([pair(st_mid)] + [pair(st_two.at[j]) for j in range(len(column_peers))])
    factor[...] = jnp.exp(st_own[:TILES, :] - peak) / total

    def probs_tile(t, carry):
        scaled = expd[t] * factor[pl.ds(t, 1), :]
        row = lax.broadcasted_iota(jnp.int32, (Z_HI * sz.share, sz.tile), 0)
        column = jnp.where(row < sz.share, row, row + PLANE * sz.columns - sz.share)
        lanes = pl.ds(pl.multiple_of(t * sz.tile, sz.tile), sz.tile)
        for half in range(Z_HI):
            rows = slice(half * sz.share, (half + 1) * sz.share)
            plain[half, :, lanes] = scaled[rows].astype(BF16)
            for d in range(2):
                less = jnp.where(column[rows] == labels[d, pl.ds(t, 1), :], scaled[rows] - 1.0, scaled[rows])
                probs[half, d * sz.share : (d + 1) * sz.share, lanes] = less.astype(BF16)
        return carry

    lax.fori_loop(0, TILES, probs_tile, 0)

    side = sz.share // 2
    sub = side // RING_PARTS

    def rs_copy(d, slot, u):
        block = ring.at[slot, d, u]
        return pltpu.make_async_remote_copy(
            src_ref=block, dst_ref=block, send_sem=rs_send.at[d, slot, u], recv_sem=rs_recv.at[d, slot, u],
            device_id=device(dz=1 if d == 0 else NZ - 1), device_id_type=MESH,
        )

    def owner(d, k):
        return (z + NZ - 1 - k) % NZ if d == 0 else (z + 1 + k) % NZ

    def product(to):
        half, first = to // Z_LO, to % Z_LO * sz.quarter
        middle = normed[:, pl.ds(pl.multiple_of(first + sz.wide, 128), sz.middle)]
        both = jnp.dot(probs[half], middle, preferred_element_type=F32).astype(BF16)
        part_sum[to, :, sz.wide : sz.wide + sz.middle] = both[: sz.share]
        part_sum[to, :, sz.quarter :] = both[sz.share :]
        for at in (0, sz.quarter - sz.wide):
            end = normed[:, pl.ds(pl.multiple_of(first + at, 128), sz.wide)]
            part_sum[to, :, at : at + sz.wide] = jnp.dot(plain[half], end, preferred_element_type=F32).astype(BF16)

    def piece(d, k, u):
        rows = slice(d * side + u * sub, d * side + (u + 1) * sub)
        slot = owner(d, k)

        @pl.when(k == 0)
        def _():
            ring[slot, d, u] = part_sum[slot, rows, :]

        @pl.when(k > 0)
        def _():
            rs_copy(d, slot, u).wait_recv()
            ring[slot, d, u] = (ring[slot, d, u].astype(F32) + part_sum[slot, rows, :].astype(F32)).astype(BF16)

        rs_copy(d, slot, u).start()

    for d in range(2):
        product(owner(d, 0))

    def for_halves(act, *what):
        for h in range(2):
            act(h, *what)

    beside = {
        (0, 0): lambda: for_halves(second.forward_a),
        (0, 1): find_far_labels,
        (1, 0): lambda: for_halves(second.forward_b, 0),
        (1, 1): lambda: for_halves(second.across_a),
        (2, 0): lambda: far_blocks(0),
        (2, 1): lambda: for_halves(second.forward_b, -1),
        (3, 0): lambda: for_halves(second.forward_b, 1),
        (3, 1): lambda: for_halves(second.across_b, 0),
        (4, 0): lambda: for_halves(second.forward_b, 2),
        (4, 1): lambda: far_blocks(1),
        (5, 0): lambda: far_blocks(-1),
        (5, 1): lambda: (for_halves(second.across_b, -1), for_halves(second.across_b, 1)),
        (6, 0): lambda: for_halves(second.across_b, 2),
        (6, 1): lambda: far_blocks(2),
    }

    def hop(k, carry):
        for u in range(RING_PARTS):
            for d in range(2):
                piece(d, k, u)

            @pl.when(k < 2)
            def _():
                product(owner(u, k + 1))

            @pl.when(k == 2)
            def _():
                product(owner(0, 3) if u == 0 else z)

            for step in range(NZ - 1):

                @pl.when(k == step)
                def _():
                    beside[step, u]()

        return carry

    lax.fori_loop(0, NZ - 1, hop, 0)

    def fin_copy(i):
        first, size, target = (
            ((1 - core) * sz.state_rows, sz.state_rows, other),
            (sz.quarter + (1 - core) * sz.middle // 2, sz.middle // 2, other_sample),
        )[i]
        return pltpu.make_async_remote_copy(
            src_ref=totals.at[pl.ds(pl.multiple_of(first, 64), size)], dst_ref=target, send_sem=fin_send.at[i],
            recv_sem=fin_recv.at[i], device_id=device(dc=1), device_id_type=MESH,
        )

    for d in range(2):
        far_turned[d] = far_sum[d].T
    for d in range(2):
        for u in range(RING_PARTS):
            rs_copy(d, z, u).wait_recv()
        rows = slice(d * side, (d + 1) * side)
        total = ring[z, d].reshape(side, sz.lanes).astype(F32) + part_sum[z, rows, :].astype(F32)
        totals[:, rows] = total.T.astype(BF16)
    for i in range(2):
        start(fin_copy(i))
    end_rows = pl.ds(pl.multiple_of(core * (sz.middle // 2), 64), sz.wide)
    middle_rows = pl.ds(pl.multiple_of((1 - core) * sz.wide, 64), sz.middle // 2)

    def place(sums, sampled, columns):
        mine_out[0, middle_rows, columns] = sums[middle_rows, :]
        mine_out[1, middle_rows, columns] = sampled[...]
        for d in range(2):
            mine_out[d, end_rows, columns] = (sums[end_rows, :].astype(F32) - far_turned[d, :, columns]).astype(BF16)

    own_sums = totals.at[pl.ds(pl.multiple_of(core * sz.state_rows, 64), sz.state_rows)]
    own_sample = totals.at[pl.ds(pl.multiple_of(sz.quarter + core * sz.middle // 2, 64), sz.middle // 2)]
    place(own_sums, own_sample, share)
    for i in range(2):
        fin_copy(i).wait_recv()
    place(other, other_sample, pl.ds(pl.multiple_of((1 - core) * sz.share, sz.share), sz.share))

    near.wait_sends()
    second.wait_sends()
    for copy in sent:
        copy.wait_send()
    w_finish()

    def drain(k, carry):
        for d in range(2):
            for u in range(RING_PARTS):
                rs_copy(d, owner(d, k), u).wait_send()
        return carry

    lax.fori_loop(0, NZ - 1, drain, 0)


def on_device(hidden, norm_gain, input_ids, sampled_ids, head_weight, moment, curvature):
    rows, features = hidden.shape
    columns = head_weight.shape[1]
    sz = Sizes(rows, features, columns, moment.shape[0])
    lanes = 128
    vmem = pl.BlockSpec(memory_space=pltpu.VMEM)
    dma = pltpu.SemaphoreType.DMA
    n_chunks = sz.weight_chunks // 2
    sums = pl.pallas_call(
        lambda *refs: kernel(sz, *refs),
        out_shape=jax.ShapeDtypeStruct((2, *moment.shape), BF16),
        in_specs=[vmem, vmem, vmem, vmem, pl.BlockSpec(memory_space=pl.ANY)],
        out_specs=vmem,
        scratch_shapes=[
            pltpu.VMEM((sz.tokens, features), BF16),
            pltpu.VMEM((Z_HI, features, sz.share), BF16),
            pltpu.VMEM((columns, features), BF16),
            pltpu.VMEM((TILES, columns, sz.tile), F32),
            pltpu.VMEM((Z_HI, 2 * sz.share, sz.tokens), BF16),
            pltpu.VMEM((Z_HI, sz.share, sz.tokens), BF16),
            pltpu.VMEM((NZ, 2, RING_PARTS, sz.share // 2 // RING_PARTS, sz.lanes), BF16),
            pltpu.VMEM((NZ, sz.share, sz.lanes), BF16),
            pltpu.VMEM((sz.lanes, sz.share), BF16),
            pltpu.VMEM((sz.state_rows, sz.share), BF16),
            pltpu.VMEM((sz.middle // 2, sz.share), BF16),
            pltpu.VMEM((rows, features), BF16),
            pltpu.VMEM((sz.far_tokens, sz.wide), BF16),
            pltpu.VMEM((2, columns, sz.wide), F32),
            pltpu.VMEM((2, sz.wide, columns), F32),
            pltpu.VMEM((2, Z_HI, 2, PLANE // 2, sz.far_block), jnp.int32),
            pltpu.VMEM((2 * TILES, sz.tile), F32),
            pltpu.VMEM((7, 2 * TILES, sz.tile), F32),
            pltpu.VMEM((2 * TILES, sz.tile), F32),
            pltpu.VMEM((3, 2 * TILES, sz.tile), F32),
            pltpu.VMEM((TILES, sz.tile), F32),
            pltpu.VMEM((2, TILES, sz.tile), jnp.int32),
            dma((40,)),
            dma((2, 4, 4, 2)),
            dma((2, 16)),
            dma((2, 16)),
            dma((2, n_chunks)),
            dma((2, n_chunks)),
            dma,
            dma((7,)),
            dma((7,)),
            dma((3,)),
            dma((3,)),
            dma((2, NZ, RING_PARTS)),
            dma((2, NZ, RING_PARTS)),
            dma((2,)),
            dma((2,)),
            dma((NZ, CORES)),
            dma((NZ, CORES)),
            dma((40,)),
            dma((2, 4, 4, 2)),
        ],
        compiler_params=pltpu.CompilerParams(
            collective_id=0, has_side_effects=True, vmem_limit_bytes=60 * 1024 * 1024
        ),
    )(hidden, norm_gain.reshape(1, -1), input_ids.reshape(-1, lanes), sampled_ids.reshape(-1, lanes), head_weight)
    gradient, sample_grad = sums[0].astype(F32), sums[1].astype(F32)
    moment_new = BETA_ONE * moment.astype(F32) + (1.0 - BETA_ONE) * gradient
    curvature_new = BETA_TWO * curvature.astype(F32) + (1.0 - BETA_TWO) * sample_grad * sample_grad
    update_direction = jnp.clip(moment_new / (RHO_SCALE * curvature_new), -1.0, 1.0)
    return moment_new.astype(BF16), curvature_new.astype(BF16), update_direction.astype(BF16)


def solution(mesh):
    in_specs = (
        P(("rep", "shard"), None),
        P(),
        P(),
        P(),
        P(None, "shard"),
        P("rep", "shard"),
        P("rep", "shard"),
    )
    out_specs = (P("rep", "shard"), P("rep", "shard"), P("rep", "shard"))
    return jax.shard_map(
        on_device, mesh=mesh, in_specs=in_specs, out_specs=out_specs, check_vma=False
    )
```

```python
import jax
import jax.numpy as jnp
from jax import lax
from jax.experimental import pallas as pl
from jax.experimental.pallas import tpu as pltpu
from jax.sharding import PartitionSpec as P

EPS_NORM = 1e-05
BETA_ONE = 0.96
BETA_TWO = 0.95
RHO_SCALE = 0.05

NX = NY = 4
Z_LO, Z_HI, CORES = 4, 2, 2
NZ = Z_HI * Z_LO
PLANE = NX * NY
W_SLACK = 2
W_AHEAD = 4
RING_PARTS = 4
TILES = 2 * 4
BF16, F32 = jnp.bfloat16, jnp.float32
MESH = pl.DeviceIdType.MESH


class Sizes:
    def __init__(self, rows, features, columns, state_rows):
        self.rows = rows
        self.half = rows // 2
        self.part = rows // 4
        self.features = features
        self.columns = columns
        self.share = columns // CORES
        self.tile = 4 * CORES * self.half
        self.tokens = TILES * self.tile
        self.state_rows = state_rows
        self.quarter = CORES * state_rows
        self.weight_chunks = 16
        self.wide = 256
        self.middle = self.quarter - 2 * self.wide
        self.lanes = self.quarter + self.middle
        self.far_block = NZ // 2 * CORES * rows
        self.far_tokens = 2 * PLANE * self.far_block


def kernel(
    sz, hidden, gain, input_ids, sampled_ids, weight, mine_out,
    normed, w_buf, w_t, expd, probs, plain, ring, part_sum, totals, other, other_sample,
    own_rows, far, far_sum, far_turned, far_labels,
    st_own, st_one, st_mid, st_two, factor, labels,
    ag_send, ag_recv, sib_send, sib_recv, w_send, w_recv, w_local, s1_send, s1_recv, s2_send, s2_recv,
    rs_send, rs_recv, fin_send, fin_recv, x_send, x_recv, f_send, f_recv,
):
    rep, shard = lax.axis_index("rep"), lax.axis_index("shard")
    z_lo, core = rep // CORES, rep % CORES
    z_hi, x, y = shard // PLANE, (shard // NY) % NX, shard % NY
    z = z_hi * Z_LO + z_lo

    def device(dx=0, dy=0, dz=0, dc=0):
        xx, yy, zz, cc = (x + dx) % NX, (y + dy) % NY, (z + dz) % NZ, (core + dc) % CORES
        return ((zz % Z_LO) * CORES + cc, (zz // Z_LO) * PLANE + xx * NY + yy)

    row_peers = [(dx, dc) for dx in range(NX) for dc in range(CORES) if (dx, dc) != (0, 0)]
    column_peers = [1, 2, 3]
    barrier = pltpu.get_barrier_semaphore()
    partners = [device(dx=dx, dc=dc) for dx, dc in row_peers]
    partners += [device(dy=dy) for dy in column_peers]
    partners += [device(dz=dz, dc=dc) for dz in range(1, NZ) for dc in range(CORES)]
    for partner in partners:
        pl.semaphore_signal(barrier, inc=1, device_id=partner, device_id_type=MESH)

    def block_row(h, da, db, cc):
        a, b = (x, y) if h == 0 else (y, x)
        return ((h * 4 + (b + db) % 4) * 4 + (a + da) % 4) * (CORES * sz.half) + cc * sz.half

    share = pl.ds(pl.multiple_of(core * sz.share, sz.share), sz.share)
    w_copy = pltpu.make_async_copy(weight.at[:, share], w_buf.at[z_hi], w_local)
    w_copy.start()

    for h in range(2):
        values = hidden[pl.ds(h * sz.half, sz.half), :].astype(F32)
        scale = lax.rsqrt(jnp.mean(values * values, axis=-1, keepdims=True) + EPS_NORM)
        rows = pl.ds(pl.multiple_of(block_row(h, 0, 0, core), sz.half), sz.half)
        block = (values * scale * gain[...]).astype(BF16)
        normed[rows, :] = block
        own_rows[h * sz.half : (h + 1) * sz.half, :] = block
    far_sum[...] = jnp.zeros_like(far_sum)
    pl.semaphore_wait(barrier, len(partners))

    sent = []

    def start(copy):
        copy.start()
        sent.append(copy)

    class Gather:
        def __init__(self, buffer, first_row, size, send_sems, recv_sems, on_arrival):
            self.buffer, self.first_row, self.size = buffer, first_row, size
            self.send_sems, self.recv_sems, self.on_arrival = send_sems, recv_sems, on_arrival
            self.sends = []

        def block(self, h, da, db, part):
            first = self.first_row(h, da, db)
            if part is None:
                return self.buffer.at[pl.ds(pl.multiple_of(first, self.size), self.size)]
            size = self.size // 2
            return self.buffer.at[pl.ds(pl.multiple_of(first + part * size, size), size)]

        def copy(self, index, h, da, db, part, along, step):
            to_a, to_b = (step, 0) if along == 0 else (0, step)
            dx, dy = (to_a, to_b) if h == 0 else (to_b, to_a)
            block = self.block(h, da, db, part)
            return pltpu.make_async_remote_copy(
                src_ref=block, dst_ref=block, send_sem=self.send_sems.at[index],
                recv_sem=self.recv_sems.at[h, (da - to_a) % 4, (db - to_b) % 4, part or 0],
                device_id=device(dx=dx, dy=dy), device_id_type=MESH,
            )

        def send(self, *what):
            self.copy(len(self.sends), *what).start()
            self.sends.append(what)

        def wait_sends(self):
            for index, what in enumerate(self.sends):
                self.copy(index, *what).wait_send()

        def wait(self, h, da, db):
            split = da % 4 == 2 if db % 4 == 0 else db % 4 == 2
            for part in (0, 1) if split else (None,):
                block = self.block(h, da, db, part)
                pltpu.make_async_remote_copy(
                    src_ref=block, dst_ref=block, send_sem=self.send_sems.at[0],
                    recv_sem=self.recv_sems.at[h, da % 4, db % 4, part or 0],
                    device_id=device(dx=1), device_id_type=MESH,
                ).wait_recv()

        def begin(self, along):
            for h in range(2):
                for step in (1, -1):
                    self.send(h, 0, 0, None, along, step)

        def forward_a(self, h):
            for da in (-1, 1):
                self.wait(h, da, 0)
                self.send(h, da, 0, 0 if da == -1 else 1, 0, -da)
            for da in (-1, 1):
                for step in (1, -1):
                    self.send(h, da, 0, None, 1, step)
                self.on_arrival(h, da, 0)

        def across_a(self, h):
            self.wait(h, 2, 0)
            for step in (1, -1):
                self.send(h, 2, 0, None, 1, step)
            self.on_arrival(h, 2, 0)

        def forward_b(self, h, da):
            for db in (-1, 1):
                self.wait(h, da, db)
                self.send(h, da, db, 0 if db == -1 else 1, 1, -db)
                self.on_arrival(h, da, db)

        def across_b(self, h, da):
            self.wait(h, da, 2)
            self.on_arrival(h, da, 2)

    def sib_copy(h, da, db, cc):
        rows = pl.ds(pl.multiple_of(block_row(h, da, db, cc), sz.half), sz.half)
        return pltpu.make_async_remote_copy(
            src_ref=normed.at[rows], dst_ref=normed.at[rows], send_sem=sib_send.at[h, (da % 4) * 4 + db % 4],
            recv_sem=sib_recv.at[h, (da % 4) * 4 + db % 4], device_id=device(dc=1), device_id_type=MESH,
        )

    def to_sibling(h, da, db):
        start(sib_copy(h, da, db, core))

    chunk = sz.features // sz.weight_chunks
    up_chunks = sz.weight_chunks // 2

    def w_copy_of(way, j, half):
        rows = pl.ds(pl.multiple_of((way * up_chunks + j) * chunk, chunk), chunk)
        block = w_buf.at[half, rows]
        return pltpu.make_async_remote_copy(
            src_ref=block, dst_ref=block, send_sem=w_send.at[way, j], recv_sem=w_recv.at[way, j],
            device_id=device(dz=1 if way == 0 else NZ - 1), device_id_type=MESH,
        )

    ends = [Z_LO - 1, 0]

    def w_first():
        for way in range(2):

            @pl.when(z_lo == ends[way])
            def _():
                for j in range(W_AHEAD):
                    w_copy_of(way, j, z_hi).start()

    def w_step(beat):
        for way in range(2):
            j = beat - W_SLACK * (z_lo if way == 0 else Z_LO - 1 - z_lo)

            @pl.when((j >= 0) & (j < up_chunks))
            def _():
                w_copy_of(way, j, 1 - z_hi).wait_recv()

                @pl.when(z_lo != ends[way])
                def _():
                    w_copy_of(way, j, 1 - z_hi).start()

            if beat + W_AHEAD < up_chunks:

                @pl.when(z_lo == ends[way])
                def _():
                    w_copy_of(way, beat, z_hi).wait_send()
                    w_copy_of(way, beat + W_AHEAD, z_hi).start()

    def w_finish():
        for way in range(2):
            for j in range(up_chunks):
                if j < up_chunks - W_AHEAD:

                    @pl.when(z_lo != ends[way])
                    def _():
                        w_copy_of(way, j, z_hi).wait_send()
                else:
                    w_copy_of(way, j, z_hi).wait_send()

    def find_labels():
        lanes = input_ids.shape[1]
        span = NX * NY * sz.rows // lanes
        first_col = (shard % PLANE) * sz.columns + core * sz.share
        row = lax.broadcasted_iota(jnp.int32, (span, lanes), 0)
        lane = lax.broadcasted_iota(jnp.int32, (span, lanes), 1)
        found = [[], []]
        for cc in range(CORES):
            block = (z_lo * CORES + cc) * Z_HI + z_hi
            now = pl.ds(pl.multiple_of(block * span, span), span)
            later = pl.ds(pl.multiple_of((block + 1) % (NZ * CORES) * span, span), span)
            ids = input_ids[now, :]
            up = jnp.concatenate([ids[1:], input_ids[later, :][:1]], axis=0)
            following = jnp.where(lane == lanes - 1, pltpu.roll(up, lanes - 1, 1), pltpu.roll(ids, lanes - 1, 1))
            last = (z_hi == Z_HI - 1) & (row == span - 1) & (lane == lanes - 1)
            found[0].append(jnp.where(last, -1, following) - first_col)
            found[1].append(sampled_ids[now, :] - first_col)
        for d in range(2):
            for h in range(2):
                for b in range(4):
                    pieces = []
                    for a in range(4):
                        xx, yy = (a, b) if h == 0 else (b, a)
                        at = (xx * NY + yy) * sz.rows + h * sz.half
                        for cc in range(CORES):
                            pieces.append(found[d][cc][at // lanes : at // lanes + 1, at % lanes : at % lanes + sz.half])
                    labels[d, h * 4 + b : h * 4 + b + 1, :] = jnp.concatenate(pieces, axis=1)

    def logits_tile(t):
        rows = pl.ds(pl.multiple_of(t * sz.tile, sz.tile), sz.tile)
        logits = lax.dot_general(
            w_t[...], normed[rows, :], (((1,), (1,)), ((), ())), preferred_element_type=F32
        )
        peak = jnp.max(logits, axis=0, keepdims=True)
        scaled = jnp.exp(logits - peak)
        expd[t] = scaled
        st_own[pl.ds(t, 1), :] = peak
        st_own[pl.ds(TILES + t, 1), :] = jnp.sum(scaled, axis=0, keepdims=True)

    def two_tiles(offset):
        for h in range(2):
            for da in range(4):
                sib_copy(h, da, offset, core).wait_recv()

        def body(h, carry):
            logits_tile(h * 4 + jnp.where(h == 0, y + offset, x + offset) % 4)
            return carry

        lax.fori_loop(0, 2, body, 0)

    near = Gather(normed, lambda h, da, db: block_row(h, da, db, core), sz.half, ag_send, ag_recv, to_sibling)
    near.begin(0)
    w_copy.wait()
    w_first()
    near.begin(1)
    for h in range(2):
        to_sibling(h, 0, 0)

    beats = iter(range(up_chunks + W_SLACK * (Z_LO - 1)))

    def w_beats(many):
        for _ in range(many):
            w_step(next(beats))

    slab = sz.columns

    def turn(half):
        def body(j, carry):
            first = pl.multiple_of(j * slab, slab)
            rows = pl.ds(pl.multiple_of(half * sz.share, sz.share), sz.share)
            w_t[rows, pl.ds(first, slab)] = w_buf[half, pl.ds(first, slab), :].T
            return carry

        lax.fori_loop(0, sz.features // slab, body, 0)

    def far_row(h, da, db):
        a, b = (x, y) if h == 0 else (y, x)
        return ((h * 4 + (b + db) % 4) * 4 + (a + da) % 4) * sz.far_block

    def far_lanes(dz, dc):
        first = (z + dz) % NZ % Z_LO * sz.quarter + (core + dc) % CORES * (sz.quarter - sz.wide)
        return pl.ds(pl.multiple_of(first, 128), sz.wide)

    def far_own(zz, cc):
        place = jnp.where(zz // Z_LO == 0, y * 4 + x, x * 4 + y)
        first = (zz // Z_LO * PLANE + place) * sz.far_block + (zz % Z_LO * CORES + cc) * sz.rows
        return pl.ds(pl.multiple_of(first, sz.rows), sz.rows)

    offsets = [(dz, dc) for dz in range(NZ) for dc in range(CORES) if (dz, dc) != (0, 0)]

    def exchange(dz, dc):
        return pltpu.make_async_remote_copy(
            src_ref=own_rows.at[:, far_lanes(dz, dc)], dst_ref=far.at[far_own(z, core)],
            send_sem=x_send.at[dz, dc], recv_sem=x_recv.at[dz, dc],
            device_id=device(dz=dz, dc=dc), device_id_type=MESH,
        )

    def exchange_start():
        for dz, dc in offsets:
            start(exchange(dz, dc))
        far[far_own(z, core), :] = own_rows[:, far_lanes(0, 0)]

    def exchange_wait():
        for dz, dc in offsets:
            exchange(dz, dc).wait_recv()

    second = Gather(far, far_row, sz.far_block, f_send, f_recv, lambda h, da, db: None)

    def find_far_labels():
        lanes = input_ids.shape[1]
        rows = input_ids.shape[0]
        span = rows // (NZ * CORES)
        ids = input_ids[...]
        row = lax.broadcasted_iota(jnp.int32, (rows, lanes), 0)
        lane = lax.broadcasted_iota(jnp.int32, (rows, lanes), 1)
        up = jnp.concatenate([ids[1:], ids[:1]], axis=0)
        following = jnp.where(lane == lanes - 1, pltpu.roll(up, lanes - 1, 1), pltpu.roll(ids, lanes - 1, 1))
        last = (row % (Z_HI * span) == Z_HI * span - 1) & (lane == lanes - 1)
        for d, found in enumerate((jnp.where(last, -1, following), sampled_ids[...])):
            found = found - shard * sz.columns
            for h in range(Z_HI):
                for odd in range(2):
                    pieces = []
                    for rr in range(Z_LO * CORES):
                        first = (rr * Z_HI + h) * span
                        pieces.append(found[first : first + span, odd * sz.rows : (odd + 1) * sz.rows])
                    far_labels[d, h, odd] = jnp.concatenate(pieces, axis=1)

    def far_blocks(offset):
        def body(i, carry):
            h, a = i // 4, i % 4
            b = (jnp.where(h == 0, y, x) + offset) % 4
            rows = pl.ds(pl.multiple_of((i // 4 * PLANE + b * 4 + a) * sz.far_block, sz.far_block), sz.far_block)
            place = jnp.where(h == 0, a * 4 + b, b * 4 + a)
            column = lax.broadcasted_iota(jnp.int32, (sz.columns, sz.far_block), 0)
            for d in range(2):
                hit = column == far_labels[d, h, place % 2, pl.ds(place // 2, 1), :]
                one_hot = jnp.where(hit, 1.0, 0.0).astype(BF16)
                far_sum[d] += jnp.dot(one_hot, far[rows, :], preferred_element_type=F32)
            return carry

        lax.fori_loop(0, 8, body, 0)

    turn(z_hi)
    w_beats(3)
    for h in range(2):
        near.forward_a(h)
    find_labels()
    w_beats(4)
    for h in range(2):
        near.forward_b(h, 0)
    for h in range(2):
        near.across_a(h)
    w_beats(3)
    for h in range(2):
        near.forward_b(h, -1)
        near.forward_b(h, 1)
    for h in range(2):
        near.across_b(h, 0)
    w_beats(3)
    for h in range(2):
        near.forward_b(h, 2)
    w_beats(1)
    exchange_start()
    turn(1 - z_hi)
    two_tiles(0)
    two_tiles(1)
    for h in range(2):
        near.across_b(h, -1)
        near.across_b(h, 1)
    two_tiles(-1)
    for h in range(2):
        near.across_b(h, 2)
    two_tiles(2)

    def join(pairs):
        peak = pairs[0][0]
        for other, _ in pairs[1:]:
            peak = jnp.maximum(peak, other)
        total = 0.0
        for other, part in pairs:
            total = total + part * jnp.exp(other - peak)
        return peak, total

    def pair(ref):
        return ref[:TILES, :], ref[TILES:, :]

    ones = [
        pltpu.make_async_remote_copy(
            src_ref=st_own, dst_ref=st_one.at[j], send_sem=s1_send.at[j], recv_sem=s1_recv.at[j],
            device_id=device(dx=dx, dc=dc), device_id_type=MESH,
        )
        for j, (dx, dc) in enumerate(row_peers)
    ]
    for copy in ones:
        start(copy)
    for copy in ones:
        copy.wait_recv()
    peak, total = join([pair(st_own)] + [pair(st_one.at[j]) for j in range(len(row_peers))])
    st_mid[:TILES, :] = peak
    st_mid[TILES:, :] = total
    twos = [
        pltpu.make_async_remote_copy(
            src_ref=st_mid, dst_ref=st_two.at[j], send_sem=s2_send.at[j], recv_sem=s2_recv.at[j],
            device_id=device(dy=dy), device_id_type=MESH,
        )
        for j, dy in enumerate(column_peers)
    ]
    for copy in twos:
        start(copy)
    exchange_wait()
    second.begin(0)
    second.begin(1)
    for copy in twos:
        copy.wait_recv()
    peak, total = join([pair(st_mid)] + [pair(st_two.at[j]) for j in range(len(column_peers))])
    factor[...] = jnp.exp(st_own[:TILES, :] - peak) / total

    def probs_tile(t, carry):
        scaled = expd[t] * factor[pl.ds(t, 1), :]
        row = lax.broadcasted_iota(jnp.int32, (Z_HI * sz.share, sz.tile), 0)
        column = jnp.where(row < sz.share, row, row + PLANE * sz.columns - sz.share)
        lanes = pl.ds(pl.multiple_of(t * sz.tile, sz.tile), sz.tile)
        for half in range(Z_HI):
            rows = slice(half * sz.share, (half + 1) * sz.share)
            plain[half, :, lanes] = scaled[rows].astype(BF16)
            for d in range(2):
                less = jnp.where(column[rows] == labels[d, pl.ds(t, 1), :], scaled[rows] - 1.0, scaled[rows])
                probs[half, d * sz.share : (d + 1) * sz.share, lanes] = less.astype(BF16)
        return carry

    lax.fori_loop(0, TILES, probs_tile, 0)

    side = sz.share // 2
    sub = side // RING_PARTS

    def rs_copy(d, slot, u):
        block = ring.at[slot, d, u]
        return pltpu.make_async_remote_copy(
            src_ref=block, dst_ref=block, send_sem=rs_send.at[d, slot, u], recv_sem=rs_recv.at[d, slot, u],
            device_id=device(dz=1 if d == 0 else NZ - 1), device_id_type=MESH,
        )

    def owner(d, k):
        return (z + NZ - 1 - k) % NZ if d == 0 else (z + 1 + k) % NZ

    def product(to):
        half, first = to // Z_LO, to % Z_LO * sz.quarter
        middle = normed[:, pl.ds(pl.multiple_of(first + sz.wide, 128), sz.middle)]
        both = jnp.dot(probs[half], middle, preferred_element_type=F32).astype(BF16)
        part_sum[to, :, sz.wide : sz.wide + sz.middle] = both[: sz.share]
        part_sum[to, :, sz.quarter :] = both[sz.share :]
        for at in (0, sz.quarter - sz.wide):
            end = normed[:, pl.ds(pl.multiple_of(first + at, 128), sz.wide)]
            part_sum[to, :, at : at + sz.wide] = jnp.dot(plain[half], end, preferred_element_type=F32).astype(BF16)

    def piece(d, k, u):
        rows = slice(d * side + u * sub, d * side + (u + 1) * sub)
        slot = owner(d, k)

        @pl.when(k == 0)
        def _():
            ring[slot, d, u] = part_sum[slot, rows, :]

        @pl.when(k > 0)
        def _():
            rs_copy(d, slot, u).wait_recv()
            ring[slot, d, u] = (ring[slot, d, u].astype(F32) + part_sum[slot, rows, :].astype(F32)).astype(BF16)

        rs_copy(d, slot, u).start()

    for d in range(2):
        product(owner(d, 0))

    def for_halves(act, *what):
        for h in range(2):
            act(h, *what)

    beside = {
        (0, 0): lambda: for_halves(second.forward_a),
        (0, 1): find_far_labels,
        (1, 0): lambda: for_halves(second.forward_b, 0),
        (1, 1): lambda: for_halves(second.across_a),
        (2, 0): lambda: far_blocks(0),
        (2, 1): lambda: for_halves(second.forward_b, -1),
        (3, 0): lambda: for_halves(second.forward_b, 1),
        (3, 1): lambda: for_halves(second.across_b, 0),
        (4, 0): lambda: for_halves(second.forward_b, 2),
        (4, 1): lambda: far_blocks(1),
        (5, 0): lambda: far_blocks(-1),
        (5, 1): lambda: (for_halves(second.across_b, -1), for_halves(second.across_b, 1)),
        (6, 0): lambda: for_halves(second.across_b, 2),
        (6, 1): lambda: far_blocks(2),
    }

    def hop(k, carry):
        for u in range(RING_PARTS):
            for d in range(2):
                piece(d, k, u)

            turn_of = u // 2
            if u % 2 == 0:

                @pl.when(k < 2)
                def _():
                    product(owner(turn_of, k + 1))

                @pl.when(k == 2)
                def _():
                    product(owner(0, 3) if turn_of == 0 else z)

            else:
                for step in range(NZ - 1):

                    @pl.when(k == step)
                    def _():
                        beside[step, turn_of]()

        return carry

    lax.fori_loop(0, NZ - 1, hop, 0)

    def fin_copy(i):
        first, size, target = (
            ((1 - core) * sz.state_rows, sz.state_rows, other),
            (sz.quarter + (1 - core) * sz.middle // 2, sz.middle // 2, other_sample),
        )[i]
        return pltpu.make_async_remote_copy(
            src_ref=totals.at[pl.ds(pl.multiple_of(first, 64), size)], dst_ref=target, send_sem=fin_send.at[i],
            recv_sem=fin_recv.at[i], device_id=device(dc=1), device_id_type=MESH,
        )

    for d in range(2):
        far_turned[d] = far_sum[d].T
    for d in range(2):
        for u in range(RING_PARTS):
            rs_copy(d, z, u).wait_recv()
        rows = slice(d * side, (d + 1) * side)
        total = ring[z, d].reshape(side, sz.lanes).astype(F32) + part_sum[z, rows, :].astype(F32)
        totals[:, rows] = total.T.astype(BF16)
    for i in range(2):
        start(fin_copy(i))
    end_rows = pl.ds(pl.multiple_of(core * (sz.middle // 2), 64), sz.wide)
    middle_rows = pl.ds(pl.multiple_of((1 - core) * sz.wide, 64), sz.middle // 2)

    def place(sums, sampled, columns):
        mine_out[0, middle_rows, columns] = sums[middle_rows, :]
        mine_out[1, middle_rows, columns] = sampled[...]
        for d in range(2):
            mine_out[d, end_rows, columns] = (sums[end_rows, :].astype(F32) - far_turned[d, :, columns]).astype(BF16)

    own_sums = totals.at[pl.ds(pl.multiple_of(core * sz.state_rows, 64), sz.state_rows)]
    own_sample = totals.at[pl.ds(pl.multiple_of(sz.quarter + core * sz.middle // 2, 64), sz.middle // 2)]
    place(own_sums, own_sample, share)
    for i in range(2):
        fin_copy(i).wait_recv()
    place(other, other_sample, pl.ds(pl.multiple_of((1 - core) * sz.share, sz.share), sz.share))

    near.wait_sends()
    second.wait_sends()
    for copy in sent:
        copy.wait_send()
    w_finish()

    def drain(k, carry):
        for d in range(2):
            for u in range(RING_PARTS):
                rs_copy(d, owner(d, k), u).wait_send()
        return carry

    lax.fori_loop(0, NZ - 1, drain, 0)


def on_device(hidden, norm_gain, input_ids, sampled_ids, head_weight, moment, curvature):
    rows, features = hidden.shape
    columns = head_weight.shape[1]
    sz = Sizes(rows, features, columns, moment.shape[0])
    lanes = 128
    vmem = pl.BlockSpec(memory_space=pltpu.VMEM)
    dma = pltpu.SemaphoreType.DMA
    n_chunks = sz.weight_chunks // 2
    sums = pl.pallas_call(
        lambda *refs: kernel(sz, *refs),
        out_shape=jax.ShapeDtypeStruct((2, *moment.shape), BF16),
        in_specs=[vmem, vmem, vmem, vmem, pl.BlockSpec(memory_space=pl.ANY)],
        out_specs=vmem,
        scratch_shapes=[
            pltpu.VMEM((sz.tokens, features), BF16),
            pltpu.VMEM((Z_HI, features, sz.share), BF16),
            pltpu.VMEM((columns, features), BF16),
            pltpu.VMEM((TILES, columns, sz.tile), F32),
            pltpu.VMEM((Z_HI, 2 * sz.share, sz.tokens), BF16),
            pltpu.VMEM((Z_HI, sz.share, sz.tokens), BF16),
            pltpu.VMEM((NZ, 2, RING_PARTS, sz.share // 2 // RING_PARTS, sz.lanes), BF16),
            pltpu.VMEM((NZ, sz.share, sz.lanes), BF16),
            pltpu.VMEM((sz.lanes, sz.share), BF16),
            pltpu.VMEM((sz.state_rows, sz.share), BF16),
            pltpu.VMEM((sz.middle // 2, sz.share), BF16),
            pltpu.VMEM((rows, features), BF16),
            pltpu.VMEM((sz.far_tokens, sz.wide), BF16),
            pltpu.VMEM((2, columns, sz.wide), F32),
            pltpu.VMEM((2, sz.wide, columns), F32),
            pltpu.VMEM((2, Z_HI, 2, PLANE // 2, sz.far_block), jnp.int32),
            pltpu.VMEM((2 * TILES, sz.tile), F32),
            pltpu.VMEM((7, 2 * TILES, sz.tile), F32),
            pltpu.VMEM((2 * TILES, sz.tile), F32),
            pltpu.VMEM((3, 2 * TILES, sz.tile), F32),
            pltpu.VMEM((TILES, sz.tile), F32),
            pltpu.VMEM((2, TILES, sz.tile), jnp.int32),
            dma((40,)),
            dma((2, 4, 4, 2)),
            dma((2, 16)),
            dma((2, 16)),
            dma((2, n_chunks)),
            dma((2, n_chunks)),
            dma,
            dma((7,)),
            dma((7,)),
            dma((3,)),
            dma((3,)),
            dma((2, NZ, RING_PARTS)),
            dma((2, NZ, RING_PARTS)),
            dma((2,)),
            dma((2,)),
            dma((NZ, CORES)),
            dma((NZ, CORES)),
            dma((40,)),
            dma((2, 4, 4, 2)),
        ],
        compiler_params=pltpu.CompilerParams(
            collective_id=0, has_side_effects=True, vmem_limit_bytes=60 * 1024 * 1024
        ),
    )(hidden, norm_gain.reshape(1, -1), input_ids.reshape(-1, lanes), sampled_ids.reshape(-1, lanes), head_weight)
    gradient, sample_grad = sums[0].astype(F32), sums[1].astype(F32)
    moment_new = BETA_ONE * moment.astype(F32) + (1.0 - BETA_ONE) * gradient
    curvature_new = BETA_TWO * curvature.astype(F32) + (1.0 - BETA_TWO) * sample_grad * sample_grad
    update_direction = jnp.clip(moment_new / (RHO_SCALE * curvature_new), -1.0, 1.0)
    return moment_new.astype(BF16), curvature_new.astype(BF16), update_direction.astype(BF16)


def solution(mesh):
    in_specs = (
        P(("rep", "shard"), None),
        P(),
        P(),
        P(),
        P(None, "shard"),
        P("rep", "shard"),
        P("rep", "shard"),
    )
    out_specs = (P("rep", "shard"), P("rep", "shard"), P("rep", "shard"))
    return jax.shard_map(
        on_device, mesh=mesh, in_specs=in_specs, out_specs=out_specs, check_vma=False
    )
```
